32 devices in a mesh: group: 4 (over x, core), shard: 8 (over z, y).
Axes of the slice: x: 2, y: 2, z: 4, core: 2. Of those that a mesh axis runs over, the one named last changes fastest.
Arguments:
- hidden: bfloat16 [2048, 8192], P('group', 'shard'), may hold values from -6 to 6
- w_x: bfloat16 [8192, 2048], P('group', 'shard'), may hold values from -0.0625 to 0.0625
- w_small: bfloat16 [8192, 2080], P('shard'), may hold values from -0.0625 to 0.0625
- conv_x: float32 [4, 2048], P(None, 'shard'), may hold values from -3 to 3
- conv_x_bias: float32 [2048], P('shard'), may hold values from -2 to 2
- conv_bc: float32 [4, 2048], replicated, may hold values from -1.5 to 1.5
- conv_bc_bias: float32 [2048], replicated, may hold values from -1 to 1
- rate: float32 [32], P('shard'), may hold values from 0.002 to 0.06
- dt_bias: float32 [32], P('shard'), may hold values from -2 to 0.5
- dskip: float32 [32], P('shard'), may hold values from 0.5 to 1.5
- old_state: float32 [16, 32, 64, 256], P('group', 'shard'), may hold values from -2 to 2
- x_tail: float32 [16, 3, 2048], P('group', None, 'shard'), may hold values from -6 to 6
- bc_tail: float32 [16, 3, 2048], P('group'), may hold values from -6 to 6
- req_count: int32 [4], replicated, may hold values from 1 to 4, as said below
- req_source: int32 [4, 4], replicated, may hold values from 0 to 15, as said below
- req_start: int32 [4, 4], replicated, may hold values from 0 to 512, as said below
Outputs:
- y_out: bfloat16 [2048, 2048], P('group', 'shard')
- new_state: float32 [16, 32, 64, 256], P('group', 'shard')
The draws below stay inside these ranges and needn't reach their ends.
Inputs may be any that keep to these rules, and one draw needn't show every extreme that they name: `req_count`: some group serves 4 requests. `req_source`: every place is named by exactly one entry; the places named by one group lie in distinct groups, so one group takes at most one request from any one group's places. `req_start`: each group's row starts with 0 and rises strictly over its first req_count entries; later entries equal 512.
All inputs are finite; a program needn't handle non-finite values.
Results may differ from the reference program's by a relative error of at most 0.006.
Values may be sent and summed in bfloat16 or wider, within the bound.
A program may use at most 128 MiB of HBM per device.

```python
import math
import jax
import jax.numpy as jnp
from jax import lax

D = 8192
P_SIZE = 64
DSTATE = 256
KCONV = 4
NGRP = 4
TOK_GRP = 512
REQ_GRP = 4
HEADS = 32
GROUPS = 4
SLOTS = 16
TOKENS = 2048


def request_plan(key):
    base_key = jax.random.fold_in(key, 7101)
    split_keys = jax.random.split(base_key, 6)
    counts = jax.random.randint(split_keys[0], (GROUPS,), 1, REQ_GRP + 1)
    fullest = jax.random.randint(split_keys[1], (), 0, GROUPS)
    counts = jnp.where(jnp.arange(GROUPS) == fullest, REQ_GRP, counts).astype(jnp.int32)

    def group_starts(sub_key, used_count):
        chosen = jax.random.permutation(sub_key, TOK_GRP - 1)[:REQ_GRP - 1] + 1
        chosen = jnp.sort(chosen).astype(jnp.int32)
        starts = jnp.concatenate([jnp.zeros((1,), jnp.int32), chosen])
        slot_ids = jnp.arange(REQ_GRP)
        return jnp.where(slot_ids < used_count, starts, TOK_GRP).astype(jnp.int32)
    starts = jax.vmap(group_starts)(jax.random.split(split_keys[2], GROUPS), counts)
    order_one = jax.random.permutation(split_keys[3], GROUPS)
    order_two = jax.random.permutation(split_keys[4], GROUPS)
    shifts = jax.random.permutation(split_keys[5], GROUPS)[:REQ_GRP]
    home_groups = order_one[(order_two[:, None] + shifts[None, :]) % GROUPS]
    sources = (home_groups * REQ_GRP + jnp.arange(REQ_GRP)[None, :]).astype(jnp.int32)
    return (counts, sources, starts)


def draw_req_count(key, part):
    return request_plan(key)[0]


def draw_req_source(key, part):
    return request_plan(key)[1]


def draw_req_start(key, part):
    return request_plan(key)[2]


def shard_levels(stream_key, dims, cuts, smallest, high):
    def one(dim, blocks):
        draws = jax.random.uniform(jax.random.fold_in(jax.random.fold_in(stream_key, 6), dim), (blocks,), jnp.float32, smallest / len(cuts), high / len(cuts))
        return jnp.repeat(jnp.exp(draws), dims[dim] // blocks).reshape((-1,) + (1,) * (len(dims) - dim - 1))

    factor_of = one(*cuts[0])
    for cut in cuts[1:]:
        factor_of = factor_of * one(*cut)
    return factor_of


def noise(stream_key, shape, scale, most, pieces=(), kind=jnp.bfloat16):
    level = shard_levels(stream_key, shape, pieces, -0.22, 0.18) if pieces else 1.0
    result = jax.random.normal(stream_key, shape, jnp.float32) * scale * level
    return jnp.minimum(jnp.maximum(result, -most), most).astype(kind)


def setup_inputs(seed: int = 0) -> dict:
    keys = jax.random.split(jax.random.key(seed), 17)
    hidden = noise(keys[0], (TOKENS, D), 1.0, 6.0, ((0, 4), (1, 8)))
    w_x = noise(keys[1], (D, HEADS * P_SIZE), D ** -0.5, 0.0625, ((0, 4), (1, 8)))
    w_small = noise(keys[2], (D, 2 * NGRP * DSTATE + HEADS), D ** -0.5, 0.0625, ((0, 8),))
    conv_x = noise(keys[3], (KCONV, HEADS * P_SIZE), KCONV ** -0.5, 3.0, ((1, 8),), jnp.float32)
    conv_x_bias = noise(keys[4], (HEADS * P_SIZE,), 0.3, 2.0, ((0, 8),), jnp.float32)
    conv_bc = noise(keys[5], (KCONV, 2 * NGRP * DSTATE), 16 ** -0.5, 1.5, (), jnp.float32)
    conv_bc_bias = noise(keys[6], (2 * NGRP * DSTATE,), 0.2, 1.0, (), jnp.float32)
    rate = jnp.clip(jnp.exp(math.log(0.06) - 3.4011973 * jax.random.uniform(keys[7], (HEADS,), jnp.float32) ** shard_levels(keys[7], (HEADS,), ((0, 8),), -0.2, 0.2)), 0.002, 0.06)
    dt_bias = jnp.clip(-2.0 + 2.5 * jax.random.uniform(keys[8], (HEADS,), jnp.float32) ** shard_levels(keys[8], (HEADS,), ((0, 8),), -0.2, 0.2), -2.0, 0.5)
    dskip = jnp.clip(0.5 + 1.0 * jax.random.uniform(keys[9], (HEADS,), jnp.float32) ** shard_levels(keys[9], (HEADS,), ((0, 8),), -0.2, 0.2), 0.5, 1.5)
    old_state = noise(keys[10], (SLOTS, HEADS, P_SIZE, DSTATE), 0.3, 2.0, ((0, 4), (1, 8)), jnp.float32)
    x_tail = noise(keys[11], (SLOTS, KCONV - 1, HEADS * P_SIZE), 1.0, 6.0, ((0, 4), (2, 8)), jnp.float32)
    bc_tail = noise(keys[12], (SLOTS, KCONV - 1, 2 * NGRP * DSTATE), 1.0, 6.0, ((0, 4),), jnp.float32)
    req_count = draw_req_count(jax.random.fold_in(keys[16], 71), 0)
    req_source = draw_req_source(jax.random.fold_in(keys[16], 71), 0)
    req_start = draw_req_start(jax.random.fold_in(keys[16], 71), 0)
    return dict(hidden=hidden, w_x=w_x, w_small=w_small, conv_x=conv_x, conv_x_bias=conv_x_bias, conv_bc=conv_bc, conv_bc_bias=conv_bc_bias, rate=rate, dt_bias=dt_bias, dskip=dskip, old_state=old_state, x_tail=x_tail, bc_tail=bc_tail, req_count=req_count, req_source=req_source, req_start=req_start)


highest_mode = lax.Precision.HIGHEST


def token_requests(starts, length):
    positions = jnp.arange(length, dtype=jnp.int32)
    return (jnp.sum((starts[None, :] <= positions[:, None]).astype(jnp.int32), axis=1) - 1).astype(jnp.int32)


def causal_conv(signal, tail_vals, starts, req_tok, kernel, shift_bias):
    length = signal.shape[0]
    positions = jnp.arange(length, dtype=jnp.int32)
    own_start = jnp.take(starts, req_tok)
    tok_tail = jnp.take(tail_vals, req_tok, axis=0)
    values = signal.astype(jnp.float32)
    summed = kernel[KCONV - 1] * values
    tail_index = jnp.arange(KCONV - 1, dtype=jnp.int32)
    for lag_steps in range(1, KCONV):
        shifted = jnp.concatenate([jnp.zeros((lag_steps, values.shape[1]), jnp.float32), values[:-lag_steps]], axis=0)
        before = own_start - (positions - lag_steps)
        select = (tail_index[None, :] == (KCONV - 1 - before)[:, None]).astype(jnp.float32)
        from_tail = jnp.sum(tok_tail * select[:, :, None], axis=1)
        summed = summed + kernel[KCONV - 1 - lag_steps] * jnp.where((before > 0)[:, None], from_tail, shifted)
    return jax.nn.silu(summed + shift_bias)


def ssd_head(x_head, dt_head, rate_head, skip_head, h_head, scores, c_wide, b_wide, req_tok, starts, req_total):
    length = x_head.shape[0]
    positions = jnp.arange(length, dtype=jnp.int32)
    log_decay = -rate_head * dt_head
    cumul = jnp.cumsum(log_decay)
    cum_before = cumul - log_decay
    inside = (req_tok[:, None] == req_tok[None, :]) & (positions[:, None] >= positions[None, :])
    decay_mat = jnp.where(inside, jnp.exp(jnp.where(inside, cumul[:, None] - cumul[None, :], 0.0)), 0.0)
    mixing = (scores * decay_mat * dt_head[None, :]).astype(jnp.bfloat16)
    local_out = jnp.dot(mixing, x_head, preferred_element_type=jnp.float32)
    slot_ids = jnp.arange(REQ_GRP, dtype=jnp.int32)
    member = req_tok[None, :] == slot_ids[:, None]
    carried = jnp.einsum("tn,kpn->ktp", c_wide, h_head, precision=highest_mode)
    carry_tok = jnp.sum(jnp.where(member[:, :, None], carried, 0.0), axis=0)
    own_start = jnp.take(starts, req_tok)
    init_decay = jnp.exp(cumul - jnp.take(cum_before, own_start))
    x_wide = x_head.astype(jnp.float32)
    y_head = local_out + init_decay[:, None] * carry_tok + skip_head * x_wide
    next_start = jnp.concatenate([starts[1:], jnp.full((1,), length, jnp.int32)])
    last_index = (jnp.minimum(next_start, length) - 1).astype(jnp.int32)
    first_index = jnp.minimum(starts, length - 1).astype(jnp.int32)
    cum_end = jnp.take(cumul, last_index)
    weights = jnp.where(member, jnp.exp(jnp.where(member, cum_end[:, None] - cumul[None, :], 0.0)), 0.0) * dt_head[None, :]
    weighted = weights[:, :, None] * x_wide[None, :, :]
    gained = jnp.einsum("ktp,tn->kpn", weighted, b_wide, precision=highest_mode)
    total_decay = jnp.exp(cum_end - jnp.take(cum_before, first_index))
    new_head = total_decay[:, None, None] * h_head + gained
    return y_head, jnp.where((slot_ids < req_total)[:, None, None], new_head, 0.0)


def reference(hidden, w_x, w_small, conv_x, conv_x_bias, conv_bc, conv_bc_bias, rate, dt_bias, dskip, old_state, x_tail, bc_tail, req_count, req_source, req_start):
    heads_grp = HEADS // NGRP
    bc_width = 2 * NGRP * DSTATE

    def one_group(group_index):
        group_rows = lax.dynamic_slice_in_dim(hidden, group_index * TOK_GRP, TOK_GRP, 0)
        x_pre = jnp.dot(group_rows, w_x, preferred_element_type=jnp.float32).astype(jnp.bfloat16)
        small_proj = jnp.dot(group_rows, w_small, preferred_element_type=jnp.float32)
        sources = req_source[group_index]
        starts = req_start[group_index]
        req_total = req_count[group_index]
        h_served = jnp.take(old_state, sources, axis=0)
        x_served = jnp.take(x_tail, sources, axis=0)
        bc_served = jnp.take(bc_tail, sources, axis=0)
        req_tok = token_requests(starts, TOK_GRP)
        x_conv = causal_conv(x_pre, x_served, starts, req_tok, conv_x, conv_x_bias).astype(jnp.bfloat16)
        dt_all = jax.nn.softplus(small_proj[:, bc_width:] + dt_bias[None, :])
        y_parts = []
        state_parts = []
        for bc_group in range(NGRP):
            b_low = bc_group * DSTATE
            c_low = NGRP * DSTATE + bc_group * DSTATE
            b_conv = causal_conv(small_proj[:, b_low:b_low + DSTATE], bc_served[:, :, b_low:b_low + DSTATE], starts, req_tok, conv_bc[:, b_low:b_low + DSTATE], conv_bc_bias[b_low:b_low + DSTATE]).astype(jnp.bfloat16)
            c_conv = causal_conv(small_proj[:, c_low:c_low + DSTATE], bc_served[:, :, c_low:c_low + DSTATE], starts, req_tok, conv_bc[:, c_low:c_low + DSTATE], conv_bc_bias[c_low:c_low + DSTATE]).astype(jnp.bfloat16)
            scores = jnp.dot(c_conv, b_conv.T, preferred_element_type=jnp.float32)
            head_low = bc_group * heads_grp
            x_grp = x_conv[:, head_low * P_SIZE:(head_low + heads_grp) * P_SIZE].reshape(TOK_GRP, heads_grp, P_SIZE)
            y_grp, new_grp = jax.vmap(ssd_head, in_axes=(1, 1, 0, 0, 1, None, None, None, None, None, None), out_axes=(1, 1))(
                x_grp, dt_all[:, head_low:head_low + heads_grp], rate[head_low:head_low + heads_grp],
                dskip[head_low:head_low + heads_grp], h_served[:, head_low:head_low + heads_grp], scores,
                c_conv.astype(jnp.float32), b_conv.astype(jnp.float32), req_tok, starts, req_total)
            y_parts.append(y_grp.reshape(TOK_GRP, heads_grp * P_SIZE))
            state_parts.append(new_grp)
        return jnp.concatenate(y_parts, axis=1).astype(jnp.bfloat16), jnp.concatenate(state_parts, axis=1)

    y_all, state_all = lax.map(one_group, jnp.arange(GROUPS, dtype=jnp.int32))
    return y_all.reshape(TOKENS, HEADS * P_SIZE), state_all.reshape(SLOTS, HEADS, P_SIZE, DSTATE)
```

```python
import functools

import jax
import jax.numpy as jnp
from jax import lax
from jax.experimental import pallas as pl
from jax.experimental.pallas import tpu as pltpu
from jax.sharding import PartitionSpec as P

P_SIZE = 64
DSTATE = 256
KCONV = 4
HEAD_DEV = 4
NGRP = 4
REQ_GRP = 4
LANES = 128
STATE_ROWS = HEAD_DEV * P_SIZE
TAIL_ROWS = 16

highest_mode = lax.Precision.HIGHEST


def dot_f32(a, b, precision=None):
    return jnp.dot(a, b, preferred_element_type=jnp.float32, precision=precision)


def split_bf16(value):
    high = value.astype(jnp.bfloat16)
    low = (value - high.astype(jnp.float32)).astype(jnp.bfloat16)
    return high, low


def head_lanes(parts, lane_head):
    out = parts[0]
    for h in range(1, HEAD_DEV):
        out = jnp.where(lane_head == h, parts[h], out)
    return out


def ssd_kernel(
    starts_ref, total_ref, origin_ref,
    x_ref, b_ref, c_ref, dt_ref, taps_ref, head_ref, skip_ref, served_ref,
    y_ref, new_ref, conv_s, mix_s,
):
    length = x_ref.shape[0]
    starts = [starts_ref[k] for k in range(REQ_GRP)]
    tok = lax.broadcasted_iota(jnp.int32, (length, 1), 0)
    own = jnp.zeros((length, 1), jnp.int32)
    for k in range(1, REQ_GRP):
        own = jnp.where(tok >= starts[k], starts[k], own)
    place = tok - own
    slot = lax.broadcasted_iota(jnp.int32, (length, TAIL_ROWS), 1)
    hot = jnp.zeros((length, TAIL_ROWS), jnp.float32)
    for k in range(REQ_GRP):
        for i in range(KCONV - 1):
            hot = jnp.where((slot == 3 * k + i) & (tok == starts[k] + i) & (place == i), 1.0, hot)
    convs = []
    for block, ref in enumerate((x_ref, b_ref, c_ref)):
        cols = slice(block * DSTATE, (block + 1) * DSTATE)
        values = ref[...].astype(jnp.float32)
        taps = [taps_ref[j : j + 1, cols] for j in range(KCONV)]
        rows = []
        for k in range(REQ_GRP):
            tail = served_ref[origin_ref[k], pl.ds(STATE_ROWS + 8 * block, 8), :]
            for i in range(KCONV - 1):
                row = jnp.zeros((1, DSTATE), jnp.float32)
                for lag in range(i + 1, KCONV):
                    at = KCONV - 1 - lag + i
                    row = row + taps[KCONV - 1 - lag] * tail[at : at + 1]
                rows.append(row)
        rows.append(jnp.zeros((TAIL_ROWS - len(rows), DSTATE), jnp.float32))
        summed = taps[KCONV - 1] * values + dot_f32(hot, jnp.concatenate(rows, 0), highest_mode)
        for lag in range(1, KCONV):
            shifted = pltpu.roll(values, lag, 0)
            summed = summed + taps[KCONV - 1 - lag] * jnp.where(place >= lag, shifted, 0.0)
        summed = summed + taps_ref[KCONV : KCONV + 1, cols]
        conv_s[block] = (summed * jax.nn.sigmoid(summed)).astype(jnp.bfloat16)
    x_conv, b_conv, c_conv = conv_s[0], conv_s[1], conv_s[2]
    x_wide = x_conv.astype(jnp.float32)
    pre = dt_ref[...] + head_ref[1:2, :]
    dt = jnp.maximum(pre, 0.0) + jnp.log1p(jnp.exp(-jnp.abs(pre)))
    a = -head_ref[0:1, :] * dt
    seq = lax.broadcasted_iota(jnp.int32, (length, length), 1)
    row_id = lax.broadcasted_iota(jnp.int32, (length, length), 0)
    inside = (seq >= own) & (seq <= row_id)
    cum = dot_f32(jnp.where(inside, 1.0, 0.0), a, highest_mode)
    member_row = lax.broadcasted_iota(jnp.int32, (8, length), 0)
    member_tok = lax.broadcasted_iota(jnp.int32, (8, length), 1)
    ends = starts[1:] + [jnp.int32(length)]
    member = jnp.zeros((8, length), jnp.float32)
    for k in range(REQ_GRP):
        member = jnp.where(
            (member_row == k) & (member_tok >= starts[k]) & (member_tok < ends[k]), 1.0, member
        )
    total = dot_f32(member, a, highest_mode)
    total_decay = jnp.exp(total)
    own_total = jnp.zeros_like(a)
    for k in range(REQ_GRP):
        own_total = jnp.where((tok >= starts[k]) & (tok < ends[k]), total[k : k + 1], own_total)
    weight = jnp.exp(own_total - cum) * dt
    init_decay = jnp.exp(cum)
    cum_t = cum.T
    dt_t = dt.T
    lane_head = lax.broadcasted_iota(jnp.int32, (1, STATE_ROWS), 1) // P_SIZE
    carry = jnp.zeros((length, STATE_ROWS), jnp.float32)
    weighted = x_wide * head_lanes([weight[:, h : h + 1] for h in range(HEAD_DEV)], lane_head)
    w_high, w_low = split_bf16(weighted.T)
    for k in range(REQ_GRP):
        held = served_ref[origin_ref[k], pl.ds(0, STATE_ROWS), :]
        h_high, h_low = split_bf16(held.T)
        mine = (tok >= starts[k]) & (tok < ends[k])
        carry = jnp.where(mine, dot_f32(c_conv, h_high) + dot_f32(c_conv, h_low), carry)
        b_mine = jnp.where(mine, b_conv.astype(jnp.float32), 0.0).astype(jnp.bfloat16)
        gained = dot_f32(w_high, b_mine) + dot_f32(w_low, b_mine)
        served = jnp.where(k < total_ref[0], 1.0, 0.0)
        for h in range(HEAD_DEV):
            rows = slice(h * P_SIZE, (h + 1) * P_SIZE)
            new_ref[k, rows, :] = served * (
                total_decay[k : k + 1, h : h + 1] * held[rows] + gained[rows]
            )
    init_wide = head_lanes([init_decay[:, h : h + 1] for h in range(HEAD_DEV)], lane_head)
    base = init_wide * carry + skip_ref[...] * x_wide
    step = 256 if length % 256 == 0 else length
    for low in range(0, length, step):
        high = low + step
        scores = lax.dot_general(
            c_conv[low:high], b_conv[:high], (((1,), (1,)), ((), ())),
            preferred_element_type=jnp.float32,
        )
        scores = jnp.where(inside[low:high, :high], scores, 0.0)
        local = jnp.zeros((step, STATE_ROWS), jnp.float32)
        for h in range(HEAD_DEV):
            decay = jnp.exp(jnp.minimum(cum[low:high, h : h + 1] - cum_t[h : h + 1, :high], 0.0))
            mixing = (scores * decay * dt_t[h : h + 1, :high]).astype(jnp.bfloat16)
            local = jnp.where(lane_head == h, dot_f32(mixing, x_conv[:high]), local)
        y_ref[low:high, :] = (local + base[low:high]).astype(jnp.bfloat16)


def ssd(starts, req_total, origin, x_pre, b_cols, c_cols, dt_cols, taps, heads, skip, served):
    length = x_pre.shape[0]
    vmem = pl.BlockSpec(memory_space=pltpu.VMEM)
    smem = pl.BlockSpec(memory_space=pltpu.SMEM)
    return pl.pallas_call(
        ssd_kernel,
        out_shape=(
            jax.ShapeDtypeStruct((length, STATE_ROWS), jnp.bfloat16),
            jax.ShapeDtypeStruct((REQ_GRP, STATE_ROWS, DSTATE), jnp.float32),
        ),
        in_specs=[smem] * 3 + [vmem] * 8,
        out_specs=(vmem, vmem),
        scratch_shapes=[
            pltpu.VMEM((3, length, DSTATE), jnp.bfloat16),
            pltpu.VMEM((8, LANES), jnp.float32),
        ],
        compiler_params=pltpu.CompilerParams(vmem_limit_bytes=48 * 2**20),
    )(starts, req_total, origin, x_pre, b_cols, c_cols, dt_cols, taps, heads, skip, served)


def tail_compute(
    starts, req_total, origin, x_pre, b_cols, c_cols, dt_cols, conv_x, conv_x_bias, conv_bc,
    conv_bc_bias, rate, dt_bias, dskip, bc_group, served,
):
    conv_all = jnp.concatenate([conv_bc, conv_bc_bias[None]], axis=0)
    b_taps = lax.dynamic_slice_in_dim(conv_all, bc_group * DSTATE, DSTATE, 1)
    c_taps = lax.dynamic_slice_in_dim(conv_all, (NGRP + bc_group) * DSTATE, DSTATE, 1)
    x_taps = jnp.concatenate([conv_x, conv_x_bias[None]], axis=0)
    taps = jnp.pad(jnp.concatenate([x_taps, b_taps, c_taps], axis=1), ((0, 3), (0, 0)))
    heads = jnp.pad(jnp.stack([rate, dt_bias]), ((0, 6), (0, LANES - HEAD_DEV)))
    skip = jnp.repeat(dskip, P_SIZE)[None]
    y, new = ssd(
        starts, req_total, origin, x_pre, b_cols, c_cols, dt_cols, taps, heads, skip, served
    )
    return y, new.reshape(REQ_GRP, HEAD_DEV, P_SIZE, DSTATE)


def packed_states(old_state, x_tail, bc_tail, req_source, bc_group):
    places = old_state.shape[0]
    me = lax.axis_index("group")
    home = req_source // places
    wanted = jnp.sum(jnp.where(home == me, req_source % places, 0), axis=1)
    b_tail = lax.dynamic_slice_in_dim(bc_tail, bc_group * DSTATE, DSTATE, 2)
    c_tail = lax.dynamic_slice_in_dim(bc_tail, (NGRP + bc_group) * DSTATE, DSTATE, 2)
    tails = [jnp.pad(t, ((0, 0), (0, 5), (0, 0))) for t in (x_tail, b_tail, c_tail)]
    flat = jnp.concatenate([old_state.reshape(places, STATE_ROWS, DSTATE)] + tails, axis=1)
    picked = [
        lax.dynamic_index_in_dim(flat, wanted[d], 0, keepdims=False)
        for d in range(wanted.shape[0])
    ]
    return jnp.stack(picked), home


def small_columns(hidden, w_small):
    length = hidden.shape[0]
    shards = lax.axis_size("shard")
    per = shards // NGRP
    width = 2 * DSTATE // per
    partial = jnp.dot(hidden, w_small, preferred_element_type=jnp.float32)
    b_part = partial[:, : NGRP * DSTATE].reshape(length, NGRP, DSTATE)
    c_part = partial[:, NGRP * DSTATE : 2 * NGRP * DSTATE].reshape(length, NGRP, DSTATE)
    bc = jnp.concatenate([b_part, c_part], axis=2).reshape(length, shards, width)
    dt = partial[:, 2 * NGRP * DSTATE :].reshape(length, shards, HEAD_DEV)
    dt_rows = jnp.transpose(dt, (1, 2, 0)).reshape(shards, HEAD_DEV * length // width, width)
    pack = jnp.concatenate([jnp.transpose(bc, (1, 0, 2)), dt_rows], axis=1)
    mine = lax.psum_scatter(pack, "shard", scatter_dimension=0, tiled=False)
    groups = [[q * per + r for r in range(per)] for q in range(NGRP)]
    both = lax.all_gather(mine[:length], "shard", axis_index_groups=groups, axis=1, tiled=True)
    dt_mine = mine[length:].reshape(HEAD_DEV, length).T
    return both[:, :DSTATE], both[:, DSTATE:], jnp.pad(dt_mine, ((0, 0), (0, LANES - HEAD_DEV)))


def body(
    hidden, w_x, w_small, conv_x, conv_x_bias, conv_bc, conv_bc_bias, rate, dt_bias, dskip,
    old_state, x_tail, bc_tail, req_count, req_source, req_start,
):
    shards = lax.axis_size("shard")
    heads_grp = HEAD_DEV * shards // NGRP
    group_index = lax.axis_index("group")
    bc_group = lax.axis_index("shard") * HEAD_DEV // heads_grp
    starts = lax.dynamic_index_in_dim(req_start, group_index, 0, keepdims=False)
    req_total = lax.dynamic_slice_in_dim(req_count, group_index, 1, 0)
    pack, home = packed_states(old_state, x_tail, bc_tail, req_source, bc_group)
    served = lax.all_to_all(pack, "group", split_axis=0, concat_axis=0, tiled=True)
    origin = lax.dynamic_index_in_dim(home, group_index, 0, keepdims=False)
    b_cols, c_cols, dt_cols = small_columns(hidden, w_small)
    panel = lax.all_gather(w_x, "group", axis=0, tiled=True)
    rows = lax.all_gather(hidden, "shard", axis=1, tiled=True)
    x_pre = jnp.dot(rows, panel, preferred_element_type=jnp.float32).astype(jnp.bfloat16)

    y, new = tail_compute(
        starts, req_total, origin, x_pre, b_cols, c_cols, dt_cols, conv_x, conv_x_bias, conv_bc,
        conv_bc_bias, rate, dt_bias, dskip, bc_group, served,
    )
    return y, new


def solution(mesh):
    in_specs = (
        P("group", "shard"),
        P("group", "shard"),
        P("shard", None),
        P(None, "shard"),
        P("shard"),
        P(),
        P(),
        P("shard"),
        P("shard"),
        P("shard"),
        P("group", "shard", None, None),
        P("group", None, "shard"),
        P("group", None, None),
        P(),
        P(),
        P(),
    )
    out_specs = (P("group", "shard"), P("group", "shard", None, None))
    return jax.shard_map(body, mesh=mesh, in_specs=in_specs, out_specs=out_specs, check_vma=False)
```

```python
import functools

import jax
import jax.numpy as jnp
from jax import lax
from jax.experimental import pallas as pl
from jax.experimental.pallas import tpu as pltpu
from jax.sharding import PartitionSpec as P

P_SIZE = 64
DSTATE = 256
KCONV = 4
HEAD_DEV = 4
NGRP = 4
REQ_GRP = 4
LANES = 128
STATE_ROWS = HEAD_DEV * P_SIZE
TAIL_ROWS = 16

highest_mode = lax.Precision.HIGHEST


def dot_f32(a, b, precision=None):
    return jnp.dot(a, b, preferred_element_type=jnp.float32, precision=precision)


def split_bf16(value):
    high = value.astype(jnp.bfloat16)
    low = (value - high.astype(jnp.float32)).astype(jnp.bfloat16)
    return high, low


def head_lanes(parts, lane_head):
    out = parts[0]
    for h in range(1, HEAD_DEV):
        out = jnp.where(lane_head == h, parts[h], out)
    return out


def ssd_kernel(
    starts_ref, total_ref, origin_ref,
    x_ref, b_ref, c_ref, dt_ref, taps_ref, head_ref, skip_ref, served_ref,
    y_ref, new_ref, conv_s,
):
    length = x_ref.shape[0]
    starts = [starts_ref[k] for k in range(REQ_GRP)]
    tok = lax.broadcasted_iota(jnp.int32, (length, 1), 0)
    own = jnp.zeros((length, 1), jnp.int32)
    for k in range(1, REQ_GRP):
        own = jnp.where(tok >= starts[k], starts[k], own)
    place = tok - own
    slot = lax.broadcasted_iota(jnp.int32, (length, TAIL_ROWS), 1)
    hot = jnp.zeros((length, TAIL_ROWS), jnp.float32)
    for k in range(REQ_GRP):
        for i in range(KCONV - 1):
            hot = jnp.where((slot == 3 * k + i) & (tok == starts[k] + i) & (place == i), 1.0, hot)
    convs = []
    for block, ref in enumerate((x_ref, b_ref, c_ref)):
        cols = slice(block * DSTATE, (block + 1) * DSTATE)
        values = ref[...].astype(jnp.float32)
        taps = [taps_ref[j : j + 1, cols] for j in range(KCONV)]
        rows = []
        for k in range(REQ_GRP):
            tail = served_ref[origin_ref[k], pl.ds(STATE_ROWS + 8 * block, 8), :]
            for i in range(KCONV - 1):
                row = jnp.zeros((1, DSTATE), jnp.float32)
                for lag in range(i + 1, KCONV):
                    at = KCONV - 1 - lag + i
                    row = row + taps[KCONV - 1 - lag] * tail[at : at + 1]
                rows.append(row)
        rows.append(jnp.zeros((TAIL_ROWS - len(rows), DSTATE), jnp.float32))
        summed = taps[KCONV - 1] * values + dot_f32(hot, jnp.concatenate(rows, 0), highest_mode)
        for lag in range(1, KCONV):
            shifted = pltpu.roll(values, lag, 0)
            summed = summed + taps[KCONV - 1 - lag] * jnp.where(place >= lag, shifted, 0.0)
        summed = summed + taps_ref[KCONV : KCONV + 1, cols]
        conv_s[block] = (summed * jax.nn.sigmoid(summed)).astype(jnp.bfloat16)
    x_conv, b_conv, c_conv = conv_s[0], conv_s[1], conv_s[2]
    x_wide = x_conv.astype(jnp.float32)
    steps = jnp.concatenate([dt_ref[...], jnp.zeros((LANES - 8, length), jnp.float32)], 0)
    pre = steps.T + head_ref[1:2, :]
    dt = jnp.maximum(pre, 0.0) + jnp.log1p(jnp.exp(-jnp.abs(pre)))
    a = -head_ref[0:1, :] * dt
    seq = lax.broadcasted_iota(jnp.int32, (length, length), 1)
    row_id = lax.broadcasted_iota(jnp.int32, (length, length), 0)
    inside = (seq >= own) & (seq <= row_id)
    cum = dot_f32(jnp.where(inside, 1.0, 0.0), a, highest_mode)
    member_row = lax.broadcasted_iota(jnp.int32, (8, length), 0)
    member_tok = lax.broadcasted_iota(jnp.int32, (8, length), 1)
    ends = starts[1:] + [jnp.int32(length)]
    member = jnp.zeros((8, length), jnp.float32)
    for k in range(REQ_GRP):
        member = jnp.where(
            (member_row == k) & (member_tok >= starts[k]) & (member_tok < ends[k]), 1.0, member
        )
    total = dot_f32(member, a, highest_mode)
    total_decay = jnp.exp(total)
    own_total = jnp.zeros_like(a)
    for k in range(REQ_GRP):
        own_total = jnp.where((tok >= starts[k]) & (tok < ends[k]), total[k : k + 1], own_total)
    weight = jnp.exp(own_total - cum) * dt
    init_decay = jnp.exp(cum)
    cum_t = cum.T
    dt_t = dt.T
    lane_head = lax.broadcasted_iota(jnp.int32, (1, STATE_ROWS), 1) // P_SIZE
    carry = jnp.zeros((length, STATE_ROWS), jnp.float32)
    weighted = x_wide * head_lanes([weight[:, h : h + 1] for h in range(HEAD_DEV)], lane_head)
    w_high, w_low = split_bf16(weighted.T)
    for k in range(REQ_GRP):
        held = served_ref[origin_ref[k], pl.ds(0, STATE_ROWS), :]
        h_high, h_low = split_bf16(held.T)
        mine = (tok >= starts[k]) & (tok < ends[k])
        carry = jnp.where(mine, dot_f32(c_conv, h_high) + dot_f32(c_conv, h_low), carry)
        b_mine = jnp.where(mine, b_conv.astype(jnp.float32), 0.0).astype(jnp.bfloat16)
        gained = dot_f32(w_high, b_mine) + dot_f32(w_low, b_mine)
        served = jnp.where(k < total_ref[0], 1.0, 0.0)
        for h in range(HEAD_DEV):
            rows = slice(h * P_SIZE, (h + 1) * P_SIZE)
            new_ref[k, rows, :] = served * (
                total_decay[k : k + 1, h : h + 1] * held[rows] + gained[rows]
            )
    init_wide = head_lanes([init_decay[:, h : h + 1] for h in range(HEAD_DEV)], lane_head)
    base = init_wide * carry + skip_ref[...] * x_wide
    step = 256 if length % 256 == 0 else length
    for low in range(0, length, step):
        high = low + step
        scores = lax.dot_general(
            c_conv[low:high], b_conv[:high], (((1,), (1,)), ((), ())),
            preferred_element_type=jnp.float32,
        )
        scores = jnp.where(inside[low:high, :high], scores, 0.0)
        local = jnp.zeros((step, STATE_ROWS), jnp.float32)
        for h in range(HEAD_DEV):
            decay = jnp.exp(jnp.minimum(cum[low:high, h : h + 1] - cum_t[h : h + 1, :high], 0.0))
            mixing = (scores * decay * dt_t[h : h + 1, :high]).astype(jnp.bfloat16)
            local = jnp.where(lane_head == h, dot_f32(mixing, x_conv[:high]), local)
        y_ref[low:high, :] = (local + base[low:high]).astype(jnp.bfloat16)


def ssd(starts, req_total, origin, x_pre, b_cols, c_cols, dt_cols, taps, heads, skip, served):
    length = x_pre.shape[0]
    vmem = pl.BlockSpec(memory_space=pltpu.VMEM)
    smem = pl.BlockSpec(memory_space=pltpu.SMEM)
    return pl.pallas_call(
        ssd_kernel,
        out_shape=(
            jax.ShapeDtypeStruct((length, STATE_ROWS), jnp.bfloat16),
            jax.ShapeDtypeStruct((REQ_GRP, STATE_ROWS, DSTATE), jnp.float32),
        ),
        in_specs=[smem] * 3 + [vmem] * 8,
        out_specs=(vmem, vmem),
        scratch_shapes=[
            pltpu.VMEM((3, length, DSTATE), jnp.bfloat16),
        ],
        compiler_params=pltpu.CompilerParams(vmem_limit_bytes=48 * 2**20),
    )(starts, req_total, origin, x_pre, b_cols, c_cols, dt_cols, taps, heads, skip, served)


def tail_compute(
    starts, req_total, origin, x_pre, b_cols, c_cols, dt_cols, conv_x, conv_x_bias, conv_bc,
    conv_bc_bias, rate, dt_bias, dskip, bc_group, served,
):
    conv_all = jnp.concatenate([conv_bc, conv_bc_bias[None]], axis=0)
    b_taps = lax.dynamic_slice_in_dim(conv_all, bc_group * DSTATE, DSTATE, 1)
    c_taps = lax.dynamic_slice_in_dim(conv_all, (NGRP + bc_group) * DSTATE, DSTATE, 1)
    x_taps = jnp.concatenate([conv_x, conv_x_bias[None]], axis=0)
    taps = jnp.pad(jnp.concatenate([x_taps, b_taps, c_taps], axis=1), ((0, 3), (0, 0)))
    heads = jnp.pad(jnp.stack([rate, dt_bias]), ((0, 6), (0, LANES - HEAD_DEV)))
    skip = jnp.repeat(dskip, P_SIZE)[None]
    y, new = ssd(
        starts, req_total, origin, x_pre, b_cols, c_cols, dt_cols, taps, heads, skip, served
    )
    return y, new.reshape(REQ_GRP, HEAD_DEV, P_SIZE, DSTATE)


def exchange_kernel(
    groups, shards, hid_ref, wx_ref, ws_ref, wdt_ref, pack_ref,
    x_out, b_out, c_out, dt_out, served_out,
    hid_in, swap_in, w_all, bc_keep, bc_send, bc_in, bcz_send, bcz_in, bc_mine, bc_other,
    xz_send, xz_in, dt_send, dt_in, served_in,
    hid_sem, swap_sem, two_sem, w_send, w_recv, bcy_s, bcy_r, bcz_s, bcz_r, fin_sem,
    xz_s, xz_r, dt_s, dt_r, st_s, st_r,
):
    g = lax.axis_index("group")
    s = lax.axis_index("shard")
    chips = groups // 2
    q, j = s // 2, s % 2
    x, c = g // 2, g % 2
    gx = (chips - 1 - x) * 2 + c
    gc = x * 2 + 1 - c
    other = q * 2 + 1 - j
    half = hid_ref.shape[1]
    root = (q % 2) == c

    def remote(src, dst, send, recv, to_g, to_s):
        return pltpu.make_async_remote_copy(
            src_ref=src, dst_ref=dst, send_sem=send, recv_sem=recv,
            device_id=(to_g, to_s), device_id_type=pl.DeviceIdType.MESH,
        )

    barrier = pltpu.get_barrier_semaphore()
    for d in range(1, shards):
        pl.semaphore_signal(
            barrier, inc=1, device_id=(g, (s + d) % shards), device_id_type=pl.DeviceIdType.MESH
        )
    for d in range(1, groups):
        pl.semaphore_signal(
            barrier, inc=1, device_id=((g + d) % groups, s), device_id_type=pl.DeviceIdType.MESH
        )
    pl.semaphore_wait(barrier, shards - 1 + groups - 1)

    keep = wx_ref.at[pl.ds(pl.multiple_of(x * half, half), half), :]
    give = wx_ref.at[pl.ds(pl.multiple_of((1 - x) * half, half), half), :]
    swap = remote(give, swap_in, swap_sem.at[0], swap_sem.at[1], gx, s)
    swap.start()
    first = remote(keep, w_all.at[x, q], two_sem.at[0], w_recv.at[x, q], g, g * 2 + j)
    second = remote(swap_in, w_all.at[x, q], two_sem.at[1], w_recv.at[x, q], g, gx * 2 + j)

    @pl.when(q != g)
    def _():
        first.start()

    width = DSTATE
    hid = hid_ref[...]

    def bc_block(side, i):
        low = pl.multiple_of((side * groups + i) * width, width)
        return dot_f32(hid, ws_ref[:, pl.ds(low, width)])

    def bcy(i):
        return remote(bc_send.at[i], bc_in.at[i], bcy_s.at[i], bcy_r.at[i], g, other)

    @pl.loop(0, groups)
    def _(i):
        bc_send[i] = bc_block(1 - j, i).astype(jnp.bfloat16)
        bcy(i).start()

    hidden_copy = remote(hid_ref, hid_in, hid_sem.at[0], hid_sem.at[1], g, other)
    hidden_copy.start()
    dt_part = lax.dot_general(
        wdt_ref[...], hid, (((1,), (1,)), ((), ())), preferred_element_type=jnp.float32
    )
    for o in range(shards):
        dt_send[o] = dt_part[o * 8 : (o + 1) * 8]

    def dt_copy(d):
        to = (s + d) % shards
        return remote(dt_send.at[to], dt_in.at[d], dt_s.at[d], dt_r.at[d], g, to)

    for d in range(1, shards):
        dt_copy(d).start()
    swap.wait_recv()

    @pl.when(q != gx)
    def _():
        second.start()

    @pl.when(q == g)
    def _():
        w_all[x, q] = wx_ref[pl.ds(pl.multiple_of(x * half, half), half), :]

    @pl.when(q == gx)
    def _():
        w_all[x, q] = swap_in[...]

    def to_chip(p):
        return remote(w_all.at[x, p], w_all.at[x, p], w_send.at[2, p], w_recv.at[x, p], gx, s)

    def to_core(u, p):
        return remote(w_all.at[u, p], w_all.at[u, p], w_send.at[u, p], w_recv.at[u, p], gc, s)

    @pl.when(root)
    def _():
        to_chip(q).start()
        to_core(x, q).start()

    def state(d):
        to = (g + d) % groups
        return remote(pack_ref.at[to], served_in.at[g], st_s.at[d], st_r.at[d], to, s)

    def state_from(d):
        frm = (g + groups - d) % groups
        return remote(pack_ref.at[frm], served_in.at[frm], st_s.at[d], st_r.at[d], frm, s)

    for d in range(1, groups):
        state(d).start()

    @pl.loop(0, groups)
    def _(i):
        bc_keep[i] = bc_block(j, i)

    def bcz(d):
        to = (q + d) % groups
        return remote(bcz_send.at[d], bcz_in.at[d], bcz_s.at[d], bcz_r.at[d], g, to * 2 + j)

    @pl.loop(0, groups)
    def _(i):
        bcy(i).wait_recv()

    @pl.loop(1, groups)
    def _(d):
        to = (q + d) % groups
        bcz_send[d] = (bc_keep[to] + bc_in[to].astype(jnp.float32)).astype(jnp.bfloat16)
        bcz(d).start()

    @pl.when(root)
    def _():
        @pl.loop(1, groups)
        def _(d):
            p = (q + groups - d) % groups
            to_core(x, p).wait_recv()
            to_chip(p).start()
            to_core(x, p).start()

        @pl.loop(0, groups)
        def _(d):
            p = (q + groups - d) % groups
            to_core(1 - x, p).wait_recv()
            to_core(1 - x, p).start()

    hidden_copy.wait_recv()

    def xz(d):
        to = (q + d) % groups
        return remote(xz_send.at[d], xz_in.at[d], xz_s.at[d], xz_r.at[d], g, to * 2 + j)

    def x_block(p):
        @pl.when(jnp.logical_not(root))
        def _():
            to_core(0, p).wait_recv()
            to_core(1, p).wait_recv()

        return dot_f32(hid_ref[...], w_all[j, p]) + dot_f32(hid_in[...], w_all[1 - j, p])

    @pl.loop(1, groups)
    def _(d):
        xz_send[d] = x_block((q + d) % groups).astype(jnp.bfloat16)
        xz(d).start()

    total = x_block(q)
    @pl.loop(1, groups)
    def _(d):
        bcz(d).wait_recv()

    mine = bc_keep[q] + bc_in[q].astype(jnp.float32)
    for d in range(1, groups):
        mine = mine + bcz_in[d].astype(jnp.float32)
    bc_mine[...] = mine
    final = remote(bc_mine, bc_other, fin_sem.at[0], fin_sem.at[1], g, other)
    final.start()
    dt_sum = dt_send[s]
    for d in range(1, shards):
        dt_copy(d).wait_recv()
        dt_sum = dt_sum + dt_in[d]
    dt_out[...] = dt_sum
    served_out[g] = pack_ref[g]
    for d in range(1, groups):
        state_from(d).wait_recv()
        frm = (g + groups - d) % groups
        served_out[frm] = served_in[frm]
    for d in range(1, groups):
        xz(d).wait_recv()
        total = total + xz_in[d].astype(jnp.float32)
    x_out[...] = total.astype(jnp.bfloat16)
    final.wait_recv()

    @pl.when(j == 0)
    def _():
        b_out[...] = bc_mine[...]
        c_out[...] = bc_other[...]

    @pl.when(j == 1)
    def _():
        b_out[...] = bc_other[...]
        c_out[...] = bc_mine[...]

    swap.wait_send()
    hidden_copy.wait_send()
    final.wait_send()

    @pl.when(q != g)
    def _():
        first.wait_send()

    @pl.when(q != gx)
    def _():
        second.wait_send()

    @pl.when(root)
    def _():
        @pl.loop(0, groups)
        def _(p):
            to_chip(p).wait_send()
            to_core(0, p).wait_send()
            to_core(1, p).wait_send()

    @pl.loop(0, groups)
    def _(i):
        bcy(i).wait_send()

    for d in range(1, groups):
        bcz(d).wait_send()
        xz(d).wait_send()
        state(d).wait_send()
    for d in range(1, shards):
        dt_copy(d).wait_send()


def exchange(groups, shards, hidden, w_x, w_small, pack):
    length, half = hidden.shape
    width = w_x.shape[1]
    bc_width = 2 * NGRP * DSTATE
    w_dt = w_small[:, bc_width:].T.reshape(shards, HEAD_DEV, half)
    w_dt = jnp.pad(w_dt, ((0, 0), (0, 8 - HEAD_DEV), (0, 0))).reshape(shards * 8, half)
    vmem = pl.BlockSpec(memory_space=pltpu.VMEM)
    bf16, f32 = jnp.bfloat16, jnp.float32
    dma = pltpu.SemaphoreType.DMA
    return pl.pallas_call(
        functools.partial(exchange_kernel, groups, shards),
        out_shape=(
            jax.ShapeDtypeStruct((length, width), bf16),
            jax.ShapeDtypeStruct((length, DSTATE), f32),
            jax.ShapeDtypeStruct((length, DSTATE), f32),
            jax.ShapeDtypeStruct((8, length), f32),
            jax.ShapeDtypeStruct(pack.shape, f32),
        ),
        in_specs=[vmem] * 5,
        out_specs=(vmem,) * 5,
        scratch_shapes=[
            pltpu.VMEM((length, half), bf16),
            pltpu.VMEM((half, width), bf16),
            pltpu.VMEM((2, groups, half, width), bf16),
            pltpu.VMEM((groups, length, DSTATE), f32),
            pltpu.VMEM((groups, length, DSTATE), bf16),
            pltpu.VMEM((groups, length, DSTATE), bf16),
            pltpu.VMEM((groups, length, DSTATE), bf16),
            pltpu.VMEM((groups, length, DSTATE), bf16),
            pltpu.VMEM((length, DSTATE), f32),
            pltpu.VMEM((length, DSTATE), f32),
            pltpu.VMEM((groups, length, width), bf16),
            pltpu.VMEM((groups, length, width), bf16),
            pltpu.VMEM((shards, 8, length), f32),
            pltpu.VMEM((shards, 8, length), f32),
            pltpu.VMEM(pack.shape, f32),
            dma((2,)), dma((2,)), dma((2,)), dma((3, groups)), dma((2, groups)),
            dma((groups,)), dma((groups,)), dma((groups,)), dma((groups,)), dma((2,)),
            dma((groups,)), dma((groups,)), dma((shards,)), dma((shards,)),
            dma((groups,)), dma((groups,)),
        ],
        compiler_params=pltpu.CompilerParams(
            collective_id=0, has_side_effects=True, vmem_limit_bytes=56 * 2**20
        ),
    )(hidden, w_x, w_small, w_dt, pack)


def packed_states(old_state, x_tail, bc_tail, req_source, bc_group):
    places = old_state.shape[0]
    me = lax.axis_index("group")
    home = req_source // places
    wanted = jnp.sum(jnp.where(home == me, req_source % places, 0), axis=1)
    b_tail = lax.dynamic_slice_in_dim(bc_tail, bc_group * DSTATE, DSTATE, 2)
    c_tail = lax.dynamic_slice_in_dim(bc_tail, (NGRP + bc_group) * DSTATE, DSTATE, 2)
    tails = [jnp.pad(t, ((0, 0), (0, 5), (0, 0))) for t in (x_tail, b_tail, c_tail)]
    flat = jnp.concatenate([old_state.reshape(places, STATE_ROWS, DSTATE)] + tails, axis=1)
    picked = [
        lax.dynamic_index_in_dim(flat, wanted[d], 0, keepdims=False)
        for d in range(wanted.shape[0])
    ]
    return jnp.stack(picked), home


def small_columns(hidden, w_small):
    length = hidden.shape[0]
    shards = lax.axis_size("shard")
    per = shards // NGRP
    width = 2 * DSTATE // per
    partial = jnp.dot(hidden, w_small, preferred_element_type=jnp.float32)
    b_part = partial[:, : NGRP * DSTATE].reshape(length, NGRP, DSTATE)
    c_part = partial[:, NGRP * DSTATE : 2 * NGRP * DSTATE].reshape(length, NGRP, DSTATE)
    bc = jnp.concatenate([b_part, c_part], axis=2).reshape(length, shards, width)
    dt = partial[:, 2 * NGRP * DSTATE :].reshape(length, shards, HEAD_DEV)
    dt_rows = jnp.transpose(dt, (1, 2, 0)).reshape(shards, HEAD_DEV * length // width, width)
    pack = jnp.concatenate([jnp.transpose(bc, (1, 0, 2)), dt_rows], axis=1)
    mine = lax.psum_scatter(pack, "shard", scatter_dimension=0, tiled=False)
    groups = [[q * per + r for r in range(per)] for q in range(NGRP)]
    both = lax.all_gather(mine[:length], "shard", axis_index_groups=groups, axis=1, tiled=True)
    dt_mine = mine[length:].reshape(HEAD_DEV, length)
    return both[:, :DSTATE], both[:, DSTATE:], jnp.pad(dt_mine, ((0, 8 - HEAD_DEV), (0, 0)))


def body(
    hidden, w_x, w_small, conv_x, conv_x_bias, conv_bc, conv_bc_bias, rate, dt_bias, dskip,
    old_state, x_tail, bc_tail, req_count, req_source, req_start,
):
    shards = lax.axis_size("shard")
    heads_grp = HEAD_DEV * shards // NGRP
    group_index = lax.axis_index("group")
    bc_group = lax.axis_index("shard") * HEAD_DEV // heads_grp
    starts = lax.dynamic_index_in_dim(req_start, group_index, 0, keepdims=False)
    req_total = lax.dynamic_slice_in_dim(req_count, group_index, 1, 0)
    pack, home = packed_states(old_state, x_tail, bc_tail, req_source, bc_group)
    origin = lax.dynamic_index_in_dim(home, group_index, 0, keepdims=False)
    groups = lax.axis_size("group")
    if groups == NGRP and shards == 2 * groups:
        x_pre, b_cols, c_cols, dt_cols, served = exchange(
            groups, shards, hidden, w_x, w_small, pack
        )
    else:
        served = lax.all_to_all(pack, "group", split_axis=0, concat_axis=0, tiled=True)
        b_cols, c_cols, dt_cols = small_columns(hidden, w_small)
        panel = lax.all_gather(w_x, "group", axis=0, tiled=True)
        rows = lax.all_gather(hidden, "shard", axis=1, tiled=True)
        x_pre = jnp.dot(rows, panel, preferred_element_type=jnp.float32).astype(jnp.bfloat16)
    y, new = tail_compute(
        starts, req_total, origin, x_pre, b_cols, c_cols, dt_cols, conv_x, conv_x_bias, conv_bc,
        conv_bc_bias, rate, dt_bias, dskip, bc_group, served,
    )
    return y, new


def solution(mesh):
    in_specs = (
        P("group", "shard"),
        P("group", "shard"),
        P("shard", None),
        P(None, "shard"),
        P("shard"),
        P(),
        P(),
        P("shard"),
        P("shard"),
        P("shard"),
        P("group", "shard", None, None),
        P("group", None, "shard"),
        P("group", None, None),
        P(),
        P(),
        P(),
    )
    out_specs = (P("group", "shard"), P("group", "shard", None, None))
    return jax.shard_map(body, mesh=mesh, in_specs=in_specs, out_specs=out_specs, check_vma=False)
```

```python
import functools

import jax
import jax.numpy as jnp
from jax import lax
from jax.experimental import pallas as pl
from jax.experimental.pallas import tpu as pltpu
from jax.sharding import PartitionSpec as P

P_SIZE = 64
DSTATE = 256
KCONV = 4
HEAD_DEV = 4
NGRP = 4
REQ_GRP = 4
LANES = 128
STATE_ROWS = HEAD_DEV * P_SIZE
TAIL_ROWS = 16

highest_mode = lax.Precision.HIGHEST


def dot_f32(a, b, precision=None):
    return jnp.dot(a, b, preferred_element_type=jnp.float32, precision=precision)


def split_bf16(value):
    high = value.astype(jnp.bfloat16)
    low = (value - high.astype(jnp.float32)).astype(jnp.bfloat16)
    return high, low


def head_lanes(parts, lane_head):
    out = parts[0]
    for h in range(1, HEAD_DEV):
        out = jnp.where(lane_head == h, parts[h], out)
    return out


def ssd_kernel(
    starts_ref, total_ref, origin_ref,
    x_ref, b_ref, c_ref, dt_ref, taps_ref, head_ref, skip_ref, served_ref,
    y_ref, new_ref, conv_s,
):
    length = x_ref.shape[0]
    starts = [starts_ref[k] for k in range(REQ_GRP)]
    tok = lax.broadcasted_iota(jnp.int32, (length, 1), 0)
    own = jnp.zeros((length, 1), jnp.int32)
    for k in range(1, REQ_GRP):
        own = jnp.where(tok >= starts[k], starts[k], own)
    place = tok - own
    slot = lax.broadcasted_iota(jnp.int32, (length, TAIL_ROWS), 1)
    hot = jnp.zeros((length, TAIL_ROWS), jnp.float32)
    for k in range(REQ_GRP):
        for i in range(KCONV - 1):
            hot = jnp.where((slot == 3 * k + i) & (tok == starts[k] + i) & (place == i), 1.0, hot)
    convs = []
    for block, ref in enumerate((x_ref, b_ref, c_ref)):
        cols = slice(block * DSTATE, (block + 1) * DSTATE)
        values = ref[...].astype(jnp.float32)
        taps = [taps_ref[j : j + 1, cols] for j in range(KCONV)]
        rows = []
        for k in range(REQ_GRP):
            tail = served_ref[origin_ref[k], pl.ds(STATE_ROWS + 8 * block, 8), :]
            for i in range(KCONV - 1):
                row = jnp.zeros((1, DSTATE), jnp.float32)
                for lag in range(i + 1, KCONV):
                    at = KCONV - 1 - lag + i
                    row = row + taps[KCONV - 1 - lag] * tail[at : at + 1]
                rows.append(row)
        rows.append(jnp.zeros((TAIL_ROWS - len(rows), DSTATE), jnp.float32))
        summed = taps[KCONV - 1] * values + dot_f32(hot, jnp.concatenate(rows, 0), highest_mode)
        for lag in range(1, KCONV):
            shifted = pltpu.roll(values, lag, 0)
            summed = summed + taps[KCONV - 1 - lag] * jnp.where(place >= lag, shifted, 0.0)
        summed = summed + taps_ref[KCONV : KCONV + 1, cols]
        conv_s[block] = (summed * jax.nn.sigmoid(summed)).astype(jnp.bfloat16)
    x_conv, b_conv, c_conv = conv_s[0], conv_s[1], conv_s[2]
    x_wide = x_conv.astype(jnp.float32)
    steps = jnp.concatenate([dt_ref[...], jnp.zeros((LANES - 8, length), jnp.float32)], 0)
    pre = steps.T + head_ref[1:2, :]
    dt = jnp.maximum(pre, 0.0) + jnp.log1p(jnp.exp(-jnp.abs(pre)))
    a = -head_ref[0:1, :] * dt
    seq = lax.broadcasted_iota(jnp.int32, (length, length), 1)
    row_id = lax.broadcasted_iota(jnp.int32, (length, length), 0)
    inside = (seq >= own) & (seq <= row_id)
    cum = dot_f32(jnp.where(inside, 1.0, 0.0), a, highest_mode)
    member_row = lax.broadcasted_iota(jnp.int32, (8, length), 0)
    member_tok = lax.broadcasted_iota(jnp.int32, (8, length), 1)
    ends = starts[1:] + [jnp.int32(length)]
    member = jnp.zeros((8, length), jnp.float32)
    for k in range(REQ_GRP):
        member = jnp.where(
            (member_row == k) & (member_tok >= starts[k]) & (member_tok < ends[k]), 1.0, member
        )
    total = dot_f32(member, a, highest_mode)
    total_decay = jnp.exp(total)
    own_total = jnp.zeros_like(a)
    for k in range(REQ_GRP):
        own_total = jnp.where((tok >= starts[k]) & (tok < ends[k]), total[k : k + 1], own_total)
    weight = jnp.exp(own_total - cum) * dt
    init_decay = jnp.exp(cum)
    cum_t = cum.T
    dt_t = dt.T
    lane_head = lax.broadcasted_iota(jnp.int32, (1, STATE_ROWS), 1) // P_SIZE
    carry = jnp.zeros((length, STATE_ROWS), jnp.float32)
    weighted = x_wide * head_lanes([weight[:, h : h + 1] for h in range(HEAD_DEV)], lane_head)
    w_high, w_low = split_bf16(weighted.T)
    for k in range(REQ_GRP):
        held = served_ref[origin_ref[k], pl.ds(0, STATE_ROWS), :]
        h_high, h_low = split_bf16(held.T)
        mine = (tok >= starts[k]) & (tok < ends[k])
        carry = jnp.where(mine, dot_f32(c_conv, h_high) + dot_f32(c_conv, h_low), carry)
        b_mine = jnp.where(mine, b_conv.astype(jnp.float32), 0.0).astype(jnp.bfloat16)
        gained = dot_f32(w_high, b_mine) + dot_f32(w_low, b_mine)
        served = jnp.where(k < total_ref[0], 1.0, 0.0)
        for h in range(HEAD_DEV):
            rows = slice(h * P_SIZE, (h + 1) * P_SIZE)
            new_ref[k, rows, :] = served * (
                total_decay[k : k + 1, h : h + 1] * held[rows] + gained[rows]
            )
    init_wide = head_lanes([init_decay[:, h : h + 1] for h in range(HEAD_DEV)], lane_head)
    base = init_wide * carry + skip_ref[...] * x_wide
    step = 256 if length % 256 == 0 else length
    for low in range(0, length, step):
        high = low + step
        scores = lax.dot_general(
            c_conv[low:high], b_conv[:high], (((1,), (1,)), ((), ())),
            preferred_element_type=jnp.float32,
        )
        scores = jnp.where(inside[low:high, :high], scores, 0.0)
        local = jnp.zeros((step, STATE_ROWS), jnp.float32)
        for h in range(HEAD_DEV):
            decay = jnp.exp(jnp.minimum(cum[low:high, h : h + 1] - cum_t[h : h + 1, :high], 0.0))
            mixing = (scores * decay * dt_t[h : h + 1, :high]).astype(jnp.bfloat16)
            local = jnp.where(lane_head == h, dot_f32(mixing, x_conv[:high]), local)
        y_ref[low:high, :] = (local + base[low:high]).astype(jnp.bfloat16)


def ssd(starts, req_total, origin, x_pre, b_cols, c_cols, dt_cols, taps, heads, skip, served):
    length = x_pre.shape[0]
    vmem = pl.BlockSpec(memory_space=pltpu.VMEM)
    smem = pl.BlockSpec(memory_space=pltpu.SMEM)
    return pl.pallas_call(
        ssd_kernel,
        out_shape=(
            jax.ShapeDtypeStruct((length, STATE_ROWS), jnp.bfloat16),
            jax.ShapeDtypeStruct((REQ_GRP, STATE_ROWS, DSTATE), jnp.float32),
        ),
        in_specs=[smem] * 3 + [vmem] * 8,
        out_specs=(vmem, vmem),
        scratch_shapes=[
            pltpu.VMEM((3, length, DSTATE), jnp.bfloat16),
        ],
        compiler_params=pltpu.CompilerParams(vmem_limit_bytes=48 * 2**20),
    )(starts, req_total, origin, x_pre, b_cols, c_cols, dt_cols, taps, heads, skip, served)


def tail_compute(
    starts, req_total, origin, x_pre, b_cols, c_cols, dt_cols, conv_x, conv_x_bias, conv_bc,
    conv_bc_bias, rate, dt_bias, dskip, bc_group, served,
):
    conv_all = jnp.concatenate([conv_bc, conv_bc_bias[None]], axis=0)
    b_taps = lax.dynamic_slice_in_dim(conv_all, bc_group * DSTATE, DSTATE, 1)
    c_taps = lax.dynamic_slice_in_dim(conv_all, (NGRP + bc_group) * DSTATE, DSTATE, 1)
    x_taps = jnp.concatenate([conv_x, conv_x_bias[None]], axis=0)
    taps = jnp.pad(jnp.concatenate([x_taps, b_taps, c_taps], axis=1), ((0, 3), (0, 0)))
    heads = jnp.pad(jnp.stack([rate, dt_bias]), ((0, 6), (0, LANES - HEAD_DEV)))
    skip = jnp.repeat(dskip, P_SIZE)[None]
    y, new = ssd(
        starts, req_total, origin, x_pre, b_cols, c_cols, dt_cols, taps, heads, skip, served
    )
    return y, new.reshape(REQ_GRP, HEAD_DEV, P_SIZE, DSTATE)


def layer_kernel(
    groups, shards, hid_ref, wx_ref, ws_ref, old_ref, xt_ref, bct_ref, cx_ref, cxb_ref, cb_ref, cbb_ref,
    rate_ref, bias_ref, dskip_ref, count_ref, source_ref, start_ref, y_ref, new_ref,
    hid_in, swap_in, w_all, bc_keep, bc_send, bc_in, bcz_send, bcz_in, bc_conv,
    xz_send, xz_in, dt_send, dt_in, pack_ref, served_in,
    hid_sem, swap_sem, two_sem, w_send, w_recv, bcy_s, bcy_r, bcz_s, bcz_r, fin_sem,
    xz_s, xz_r, dt_s, dt_r, st_s, st_r, carry_keep,
):
    g = lax.axis_index("group")
    s = lax.axis_index("shard")
    chips = groups // 2
    q, j = s // 2, s % 2
    x, c = g // 2, g % 2
    gx = (chips - 1 - x) * 2 + c
    gc = x * 2 + 1 - c
    other = q * 2 + 1 - j
    half = hid_ref.shape[1]
    root = (q % 2) == c

    def remote(src, dst, send, recv, to_g, to_s):
        return pltpu.make_async_remote_copy(
            src_ref=src, dst_ref=dst, send_sem=send, recv_sem=recv,
            device_id=(to_g, to_s), device_id_type=pl.DeviceIdType.MESH,
        )

    barrier = pltpu.get_barrier_semaphore()
    for d in range(1, shards):
        pl.semaphore_signal(
            barrier, inc=1, device_id=(g, (s + d) % shards), device_id_type=pl.DeviceIdType.MESH
        )
    for d in range(1, groups):
        pl.semaphore_signal(
            barrier, inc=1, device_id=((g + d) % groups, s), device_id_type=pl.DeviceIdType.MESH
        )
    pl.semaphore_wait(barrier, shards - 1 + groups - 1)

    keep = wx_ref.at[pl.ds(pl.multiple_of(x * half, half), half), :]
    give = wx_ref.at[pl.ds(pl.multiple_of((1 - x) * half, half), half), :]
    swap = remote(give, swap_in, swap_sem.at[0], swap_sem.at[1], gx, s)
    swap.start()
    first = remote(keep, w_all.at[x, q], two_sem.at[0], w_recv.at[x, q], g, g * 2 + j)
    second = remote(swap_in, w_all.at[x, q], two_sem.at[1], w_recv.at[x, q], g, gx * 2 + j)

    @pl.when(q != g)
    def _():
        first.start()

    width = DSTATE
    hid = hid_ref[...]

    def bc_block(side, i):
        low = pl.multiple_of((side * groups + i) * width, width)
        return lax.dot_general(
            hid, ws_ref[pl.ds(low, width), :], (((1,), (1,)), ((), ())),
            preferred_element_type=jnp.float32,
        )

    def bcy(i):
        return remote(bc_send.at[i], bc_in.at[i], bcy_s.at[i], bcy_r.at[i], g, other)

    @pl.loop(0, groups)
    def _(i):
        bc_send[i] = bc_block(1 - j, i).astype(jnp.bfloat16)
        bcy(i).start()

    hidden_copy = remote(hid_ref, hid_in, hid_sem.at[0], hid_sem.at[1], g, other)
    hidden_copy.start()
    dt_part = lax.dot_general(
        ws_ref[pl.ds(2 * NGRP * DSTATE, HEAD_DEV * shards), :], hid, (((1,), (1,)), ((), ())), preferred_element_type=jnp.float32
    )
    for o in range(shards):
        part = dt_part[o * HEAD_DEV : (o + 1) * HEAD_DEV]
        dt_send[o] = jnp.concatenate([part, jnp.zeros((8 - HEAD_DEV, part.shape[1]), jnp.float32)], 0)

    def dt_copy(d):
        to = (s + d) % shards
        return remote(dt_send.at[to], dt_in.at[d], dt_s.at[d], dt_r.at[d], g, to)

    for d in range(1, shards):
        dt_copy(d).start()
    swap.wait_recv()

    @pl.when(q != gx)
    def _():
        second.start()

    @pl.when(q == g)
    def _():
        w_all[x, q] = wx_ref[pl.ds(pl.multiple_of(x * half, half), half), :]

    @pl.when(q == gx)
    def _():
        w_all[x, q] = swap_in[...]

    def to_chip(p):
        return remote(w_all.at[x, p], w_all.at[x, p], w_send.at[2, p], w_recv.at[x, p], gx, s)

    def to_core(u, p):
        return remote(w_all.at[u, p], w_all.at[u, p], w_send.at[u, p], w_recv.at[u, p], gc, s)

    @pl.when(root)
    def _():
        to_chip(q).start()
        to_core(x, q).start()

    def state(d):
        to = (g + d) % groups
        return remote(pack_ref.at[to], served_in.at[g], st_s.at[d], st_r.at[d], to, s)

    def state_from(d):
        frm = (g + groups - d) % groups
        return remote(pack_ref.at[frm], served_in.at[frm], st_s.at[d], st_r.at[d], frm, s)

    bc_group = s * NGRP // shards
    places = old_ref.shape[0]
    for d in range(groups):
        wanted = jnp.int32(0)
        for k in range(REQ_GRP):
            named = source_ref[d, k]
            wanted = wanted + jnp.where(named // places == g, named % places, 0)
        pack_ref[d, 0:STATE_ROWS, :] = old_ref[wanted]
        pack_ref[d, STATE_ROWS : STATE_ROWS + 3, :] = xt_ref[wanted]
        for side in range(2):
            low = pl.multiple_of((side * NGRP + bc_group) * DSTATE, DSTATE)
            at = STATE_ROWS + 8 * (side + 1)
            pack_ref[d, at : at + 3, :] = bct_ref[wanted, :, pl.ds(low, DSTATE)]
        for block in range(3):
            at = STATE_ROWS + 8 * block
            pack_ref[d, at + 3 : at + 8, :] = jnp.zeros((5, DSTATE), jnp.float32)
    for d in range(1, groups):
        state(d).start()

    @pl.loop(0, groups)
    def _(i):
        bc_keep[i] = bc_block(j, i)

    def bcz(d):
        to = (q + d) % groups
        return remote(bcz_send.at[d], bcz_in.at[d], bcz_s.at[d], bcz_r.at[d], g, to * 2 + j)

    @pl.loop(0, groups)
    def _(i):
        bcy(i).wait_recv()

    @pl.loop(1, groups)
    def _(d):
        to = (q + d) % groups
        bcz_send[d] = (bc_keep[to] + bc_in[to].astype(jnp.float32)).astype(jnp.bfloat16)
        bcz(d).start()

    def pass_on(p):
        to_core(1 - x, p).wait_recv()
        to_core(1 - x, p).start()

    @pl.when(root)
    def _():
        @pl.loop(1, groups)
        def _(d):
            p = (q + groups - d) % groups
            to_core(x, p).wait_recv()
            to_chip(p).start()
            to_core(x, p).start()

        pass_on(q)

    hidden_copy.wait_recv()

    def xz(d):
        to = (q + groups - d) % groups
        return remote(xz_send.at[d], xz_in.at[d], xz_s.at[d], xz_r.at[d], g, to * 2 + j)

    def x_block(p):
        @pl.when(jnp.logical_not(root))
        def _():
            to_core(0, p).wait_recv()
            to_core(1, p).wait_recv()

        return dot_f32(hid_ref[...], w_all[j, p]) + dot_f32(hid_in[...], w_all[1 - j, p])

    @pl.loop(1, groups)
    def _(d):
        p = (q + groups - d) % groups

        @pl.when(root)
        def _():
            pass_on(p)

        xz_send[d] = x_block(p).astype(jnp.bfloat16)
        xz(d).start()

    total_x = x_block(q)
    @pl.loop(1, groups)
    def _(d):
        bcz(d).wait_recv()

    mine = bc_keep[q] + bc_in[q].astype(jnp.float32)
    for d in range(1, groups):
        mine = mine + bcz_in[d].astype(jnp.float32)
    length = hid_ref.shape[0]
    origin = [source_ref[g, k] // places for k in range(REQ_GRP)]
    starts = [start_ref[g, k] for k in range(REQ_GRP)]
    tok = lax.broadcasted_iota(jnp.int32, (length, 1), 0)
    own = jnp.zeros((length, 1), jnp.int32)
    for k in range(1, REQ_GRP):
        own = jnp.where(tok >= starts[k], starts[k], own)
    place = tok - own
    slot = lax.broadcasted_iota(jnp.int32, (length, TAIL_ROWS), 1)
    hot = jnp.zeros((length, TAIL_ROWS), jnp.float32)
    for k in range(REQ_GRP):
        for i in range(KCONV - 1):
            hot = jnp.where((slot == 3 * k + i) & (tok == starts[k] + i) & (place == i), 1.0, hot)

    def convolve(values, tap, bias, block):
        taps = [tap[i : i + 1] for i in range(KCONV)]
        rows = []
        for k in range(REQ_GRP):
            low = pl.multiple_of(STATE_ROWS + 8 * block, 8)
            tail = served_in[origin[k], pl.ds(low, 8), :]
            for i in range(KCONV - 1):
                row = jnp.zeros((1, DSTATE), jnp.float32)
                for lag in range(i + 1, KCONV):
                    at = KCONV - 1 - lag + i
                    row = row + taps[KCONV - 1 - lag] * tail[at : at + 1]
                rows.append(row)
        rows.append(jnp.zeros((TAIL_ROWS - len(rows), DSTATE), jnp.float32))
        summed = taps[KCONV - 1] * values + dot_f32(hot, jnp.concatenate(rows, 0), highest_mode)
        for lag in range(1, KCONV):
            shifted = pltpu.roll(values, lag, 0)
            summed = summed + taps[KCONV - 1 - lag] * jnp.where(place >= lag, shifted, 0.0)
        summed = summed + bias
        return (summed * jax.nn.sigmoid(summed)).astype(jnp.bfloat16)

    served_in[g] = pack_ref[g]
    for d in range(1, groups):
        state_from(d).wait_recv()
    side_cols = pl.ds(pl.multiple_of((j * NGRP + bc_group) * DSTATE, DSTATE), DSTATE)
    bc_conv[j] = convolve(mine, cb_ref[:, side_cols], cbb_ref[:, side_cols], j + 1)
    final = remote(bc_conv.at[j], bc_conv.at[j], fin_sem.at[0], fin_sem.at[1], g, other)
    final_in = remote(bc_conv.at[1 - j], bc_conv.at[1 - j], fin_sem.at[0], fin_sem.at[1], g, other)
    final.start()
    dt_sum = dt_send[s]
    for d in range(1, shards):
        dt_copy(d).wait_recv()
        dt_sum = dt_sum + dt_in[d]
    steps = jnp.concatenate([dt_sum, jnp.zeros((LANES - 8, length), jnp.float32)], 0)
    lane = lax.broadcasted_iota(jnp.int32, (1, LANES), 1)
    lane_head = lax.broadcasted_iota(jnp.int32, (1, STATE_ROWS), 1) // P_SIZE
    rate_row = jnp.zeros((1, LANES), jnp.float32)
    bias_row = jnp.zeros((1, LANES), jnp.float32)
    skip_row = jnp.zeros((1, STATE_ROWS), jnp.float32)
    for h in range(HEAD_DEV):
        rate_row = jnp.where(lane == h, rate_ref[h], rate_row)
        bias_row = jnp.where(lane == h, bias_ref[h], bias_row)
        skip_row = jnp.where(lane_head == h, dskip_ref[h], skip_row)
    pre = steps.T + bias_row
    dt = jnp.maximum(pre, 0.0) + jnp.log1p(jnp.exp(-jnp.abs(pre)))
    a = -rate_row * dt
    seq = lax.broadcasted_iota(jnp.int32, (length, length), 1)
    row_id = lax.broadcasted_iota(jnp.int32, (length, length), 0)
    inside = (seq >= own) & (seq <= row_id)
    cum = dot_f32(jnp.where(inside, 1.0, 0.0), a, highest_mode)
    member_row = lax.broadcasted_iota(jnp.int32, (8, length), 0)
    member_tok = lax.broadcasted_iota(jnp.int32, (8, length), 1)
    ends = starts[1:] + [jnp.int32(length)]
    member = jnp.zeros((8, length), jnp.float32)
    for k in range(REQ_GRP):
        member = jnp.where(
            (member_row == k) & (member_tok >= starts[k]) & (member_tok < ends[k]), 1.0, member
        )
    total = dot_f32(member, a, highest_mode)
    total_decay = jnp.exp(total)
    own_total = jnp.zeros_like(a)
    for k in range(REQ_GRP):
        own_total = jnp.where((tok >= starts[k]) & (tok < ends[k]), total[k : k + 1], own_total)
    weight = jnp.exp(own_total - cum) * dt
    init_decay = jnp.exp(cum)
    cum_t = cum.T
    dt_t = dt.T
    final_in.wait_recv()
    b_conv, c_conv = bc_conv[0], bc_conv[1]
    carry = jnp.zeros((length, STATE_ROWS), jnp.float32)
    for k in range(REQ_GRP):
        h_high, h_low = split_bf16(served_in[origin[k], pl.ds(0, STATE_ROWS), :].T)
        mine_tok = (tok >= starts[k]) & (tok < ends[k])
        carry = jnp.where(mine_tok, dot_f32(c_conv, h_high) + dot_f32(c_conv, h_low), carry)
    init_wide = head_lanes([init_decay[:, h : h + 1] for h in range(HEAD_DEV)], lane_head)
    carry_keep[...] = init_wide * carry
    for d in range(1, groups):
        xz(d).wait_recv()
        total_x = total_x + xz_in[d].astype(jnp.float32)
    x_pre = total_x.astype(jnp.bfloat16).astype(jnp.float32)
    x_conv = convolve(x_pre, cx_ref[...], cxb_ref[...], 0)
    x_wide = x_conv.astype(jnp.float32)
    weighted = x_wide * head_lanes([weight[:, h : h + 1] for h in range(HEAD_DEV)], lane_head)
    w_high, w_low = split_bf16(weighted.T)
    for k in range(REQ_GRP):
        held = served_in[origin[k], pl.ds(0, STATE_ROWS), :]
        mine = (tok >= starts[k]) & (tok < ends[k])
        b_mine = jnp.where(mine, b_conv.astype(jnp.float32), 0.0).astype(jnp.bfloat16)
        gained = dot_f32(w_high, b_mine) + dot_f32(w_low, b_mine)
        served = jnp.where(k < count_ref[g], 1.0, 0.0)
        for h in range(HEAD_DEV):
            rows = slice(h * P_SIZE, (h + 1) * P_SIZE)
            new_ref[k, rows, :] = served * (
                total_decay[k : k + 1, h : h + 1] * held[rows] + gained[rows]
            )
    base = carry_keep[...] + skip_row * x_wide
    step = 256 if length % 256 == 0 else length
    for low in range(0, length, step):
        high = low + step
        scores = lax.dot_general(
            c_conv[low:high], b_conv[:high], (((1,), (1,)), ((), ())),
            preferred_element_type=jnp.float32,
        )
        scores = jnp.where(inside[low:high, :high], scores, 0.0)
        local = jnp.zeros((step, STATE_ROWS), jnp.float32)
        for h in range(HEAD_DEV):
            decay = jnp.exp(jnp.minimum(cum[low:high, h : h + 1] - cum_t[h : h + 1, :high], 0.0))
            mixing = (scores * decay * dt_t[h : h + 1, :high]).astype(jnp.bfloat16)
            local = jnp.where(lane_head == h, dot_f32(mixing, x_conv[:high]), local)
        y_ref[low:high, :] = (local + base[low:high]).astype(jnp.bfloat16)

    swap.wait_send()
    hidden_copy.wait_send()
    final.wait_send()

    @pl.when(q != g)
    def _():
        first.wait_send()

    @pl.when(q != gx)
    def _():
        second.wait_send()

    @pl.when(root)
    def _():
        @pl.loop(0, groups)
        def _(p):
            to_chip(p).wait_send()
            to_core(0, p).wait_send()
            to_core(1, p).wait_send()

    @pl.loop(0, groups)
    def _(i):
        bcy(i).wait_send()

    for d in range(1, groups):
        bcz(d).wait_send()
        xz(d).wait_send()
        state(d).wait_send()
    for d in range(1, shards):
        dt_copy(d).wait_send()


def layer(
    groups, shards, hidden, w_x, w_small, conv_x, conv_x_bias, conv_bc, conv_bc_bias, rate,
    dt_bias, dskip, old_state, x_tail, bc_tail, req_count, req_source, req_start,
):
    length, half = hidden.shape
    width = w_x.shape[1]
    places = old_state.shape[0]
    vmem = pl.BlockSpec(memory_space=pltpu.VMEM)
    smem = pl.BlockSpec(memory_space=pltpu.SMEM)
    bf16, f32 = jnp.bfloat16, jnp.float32
    dma = pltpu.SemaphoreType.DMA
    packed = (groups, STATE_ROWS + 24, DSTATE)
    y, new = pl.pallas_call(
        functools.partial(layer_kernel, groups, shards),
        out_shape=(
            jax.ShapeDtypeStruct((length, STATE_ROWS), bf16),
            jax.ShapeDtypeStruct((REQ_GRP, STATE_ROWS, DSTATE), f32),
        ),
        in_specs=[vmem] * 10 + [smem] * 6,
        out_specs=(vmem, vmem),
        scratch_shapes=[
            pltpu.VMEM((length, half), bf16),
            pltpu.VMEM((half, width), bf16),
            pltpu.VMEM((2, groups, half, width), bf16),
            pltpu.VMEM((groups, length, DSTATE), f32),
            pltpu.VMEM((groups, length, DSTATE), bf16),
            pltpu.VMEM((groups, length, DSTATE), bf16),
            pltpu.VMEM((groups, length, DSTATE), bf16),
            pltpu.VMEM((groups, length, DSTATE), bf16),
            pltpu.VMEM((2, length, DSTATE), bf16),
            pltpu.VMEM((groups, length, width), bf16),
            pltpu.VMEM((groups, length, width), bf16),
            pltpu.VMEM((shards, 8, length), f32),
            pltpu.VMEM((shards, 8, length), f32),
            pltpu.VMEM(packed, f32),
            pltpu.VMEM(packed, f32),
            dma((2,)), dma((2,)), dma((2,)), dma((3, groups)), dma((2, groups)),
            dma((groups,)), dma((groups,)), dma((groups,)), dma((groups,)), dma((2,)),
            dma((groups,)), dma((groups,)), dma((shards,)), dma((shards,)),
            dma((groups,)), dma((groups,)),
            pltpu.VMEM((length, STATE_ROWS), f32),
        ],
        compiler_params=pltpu.CompilerParams(
            collective_id=0, has_side_effects=True, vmem_limit_bytes=58 * 2**20
        ),
    )(
        hidden, w_x, w_small.T, old_state.reshape(places, STATE_ROWS, DSTATE), x_tail, bc_tail,
        conv_x, conv_x_bias[None], conv_bc, conv_bc_bias[None], rate, dt_bias, dskip,
        req_count, req_source, req_start,
    )
    return y, new.reshape(REQ_GRP, HEAD_DEV, P_SIZE, DSTATE)


def packed_states(old_state, x_tail, bc_tail, req_source, bc_group):
    places = old_state.shape[0]
    me = lax.axis_index("group")
    home = req_source // places
    wanted = jnp.sum(jnp.where(home == me, req_source % places, 0), axis=1)
    b_tail = lax.dynamic_slice_in_dim(bc_tail, bc_group * DSTATE, DSTATE, 2)
    c_tail = lax.dynamic_slice_in_dim(bc_tail, (NGRP + bc_group) * DSTATE, DSTATE, 2)
    tails = [jnp.pad(t, ((0, 0), (0, 5), (0, 0))) for t in (x_tail, b_tail, c_tail)]
    flat = jnp.concatenate([old_state.reshape(places, STATE_ROWS, DSTATE)] + tails, axis=1)
    picked = [
        lax.dynamic_index_in_dim(flat, wanted[d], 0, keepdims=False)
        for d in range(wanted.shape[0])
    ]
    return jnp.stack(picked), home


def small_columns(hidden, w_small):
    length = hidden.shape[0]
    shards = lax.axis_size("shard")
    per = shards // NGRP
    width = 2 * DSTATE // per
    partial = jnp.dot(hidden, w_small, preferred_element_type=jnp.float32)
    b_part = partial[:, : NGRP * DSTATE].reshape(length, NGRP, DSTATE)
    c_part = partial[:, NGRP * DSTATE : 2 * NGRP * DSTATE].reshape(length, NGRP, DSTATE)
    bc = jnp.concatenate([b_part, c_part], axis=2).reshape(length, shards, width)
    dt = partial[:, 2 * NGRP * DSTATE :].reshape(length, shards, HEAD_DEV)
    dt_rows = jnp.transpose(dt, (1, 2, 0)).reshape(shards, HEAD_DEV * length // width, width)
    pack = jnp.concatenate([jnp.transpose(bc, (1, 0, 2)), dt_rows], axis=1)
    mine = lax.psum_scatter(pack, "shard", scatter_dimension=0, tiled=False)
    groups = [[q * per + r for r in range(per)] for q in range(NGRP)]
    both = lax.all_gather(mine[:length], "shard", axis_index_groups=groups, axis=1, tiled=True)
    dt_mine = mine[length:].reshape(HEAD_DEV, length)
    return both[:, :DSTATE], both[:, DSTATE:], jnp.pad(dt_mine, ((0, 8 - HEAD_DEV), (0, 0)))


def body(
    hidden, w_x, w_small, conv_x, conv_x_bias, conv_bc, conv_bc_bias, rate, dt_bias, dskip,
    old_state, x_tail, bc_tail, req_count, req_source, req_start,
):
    shards = lax.axis_size("shard")
    groups = lax.axis_size("group")
    if groups == NGRP and shards == 2 * groups:
        return layer(
            groups, shards, hidden, w_x, w_small, conv_x, conv_x_bias, conv_bc, conv_bc_bias, rate,
            dt_bias, dskip, old_state, x_tail, bc_tail, req_count, req_source, req_start,
        )
    heads_grp = HEAD_DEV * shards // NGRP
    group_index = lax.axis_index("group")
    bc_group = lax.axis_index("shard") * HEAD_DEV // heads_grp
    starts = lax.dynamic_index_in_dim(req_start, group_index, 0, keepdims=False)
    req_total = lax.dynamic_slice_in_dim(req_count, group_index, 1, 0)
    pack, home = packed_states(old_state, x_tail, bc_tail, req_source, bc_group)
    origin = lax.dynamic_index_in_dim(home, group_index, 0, keepdims=False)
    served = lax.all_to_all(pack, "group", split_axis=0, concat_axis=0, tiled=True)
    b_cols, c_cols, dt_cols = small_columns(hidden, w_small)
    panel = lax.all_gather(w_x, "group", axis=0, tiled=True)
    rows = lax.all_gather(hidden, "shard", axis=1, tiled=True)
    x_pre = jnp.dot(rows, panel, preferred_element_type=jnp.float32).astype(jnp.bfloat16)
    y, new = tail_compute(
        starts, req_total, origin, x_pre, b_cols, c_cols, dt_cols, conv_x, conv_x_bias, conv_bc,
        conv_bc_bias, rate, dt_bias, dskip, bc_group, served,
    )
    return y, new


def solution(mesh):
    in_specs = (
        P("group", "shard"),
        P("group", "shard"),
        P("shard", None),
        P(None, "shard"),
        P("shard"),
        P(),
        P(),
        P("shard"),
        P("shard"),
        P("shard"),
        P("group", "shard", None, None),
        P("group", None, "shard"),
        P("group", None, None),
        P(),
        P(),
        P(),
    )
    out_specs = (P("group", "shard"), P("group", "shard", None, None))
    return jax.shard_map(body, mesh=mesh, in_specs=in_specs, out_specs=out_specs, check_vma=False)
```

```python
import functools

import jax
import jax.numpy as jnp
from jax import lax
from jax.experimental import pallas as pl
from jax.experimental.pallas import tpu as pltpu
from jax.sharding import PartitionSpec as P

P_SIZE = 64
DSTATE = 256
KCONV = 4
HEAD_DEV = 4
NGRP = 4
REQ_GRP = 4
LANES = 128
STATE_ROWS = HEAD_DEV * P_SIZE
TAIL_ROWS = 16

highest_mode = lax.Precision.HIGHEST


def dot_f32(a, b, precision=None):
    return jnp.dot(a, b, preferred_element_type=jnp.float32, precision=precision)


def split_bf16(value):
    high = value.astype(jnp.bfloat16)
    low = (value - high.astype(jnp.float32)).astype(jnp.bfloat16)
    return high, low


def head_lanes(parts, lane_head):
    out = parts[0]
    for h in range(1, HEAD_DEV):
        out = jnp.where(lane_head == h, parts[h], out)
    return out


def ssd_kernel(
    starts_ref, total_ref, origin_ref,
    x_ref, b_ref, c_ref, dt_ref, taps_ref, head_ref, skip_ref, served_ref,
    y_ref, new_ref, conv_s,
):
    length = x_ref.shape[0]
    starts = [starts_ref[k] for k in range(REQ_GRP)]
    tok = lax.broadcasted_iota(jnp.int32, (length, 1), 0)
    own = jnp.zeros((length, 1), jnp.int32)
    for k in range(1, REQ_GRP):
        own = jnp.where(tok >= starts[k], starts[k], own)
    place = tok - own
    slot = lax.broadcasted_iota(jnp.int32, (length, TAIL_ROWS), 1)
    hot = jnp.zeros((length, TAIL_ROWS), jnp.float32)
    for k in range(REQ_GRP):
        for i in range(KCONV - 1):
            hot = jnp.where((slot == 3 * k + i) & (tok == starts[k] + i) & (place == i), 1.0, hot)
    convs = []
    for block, ref in enumerate((x_ref, b_ref, c_ref)):
        cols = slice(block * DSTATE, (block + 1) * DSTATE)
        values = ref[...].astype(jnp.float32)
        taps = [taps_ref[j : j + 1, cols] for j in range(KCONV)]
        rows = []
        for k in range(REQ_GRP):
            tail = served_ref[origin_ref[k], pl.ds(STATE_ROWS + 8 * block, 8), :]
            for i in range(KCONV - 1):
                row = jnp.zeros((1, DSTATE), jnp.float32)
                for lag in range(i + 1, KCONV):
                    at = KCONV - 1 - lag + i
                    row = row + taps[KCONV - 1 - lag] * tail[at : at + 1]
                rows.append(row)
        rows.append(jnp.zeros((TAIL_ROWS - len(rows), DSTATE), jnp.float32))
        summed = taps[KCONV - 1] * values + dot_f32(hot, jnp.concatenate(rows, 0), highest_mode)
        for lag in range(1, KCONV):
            shifted = pltpu.roll(values, lag, 0)
            summed = summed + taps[KCONV - 1 - lag] * jnp.where(place >= lag, shifted, 0.0)
        summed = summed + taps_ref[KCONV : KCONV + 1, cols]
        conv_s[block] = (summed * jax.nn.sigmoid(summed)).astype(jnp.bfloat16)
    x_conv, b_conv, c_conv = conv_s[0], conv_s[1], conv_s[2]
    x_wide = x_conv.astype(jnp.float32)
    steps = jnp.concatenate([dt_ref[...], jnp.zeros((LANES - 8, length), jnp.float32)], 0)
    pre = steps.T + head_ref[1:2, :]
    dt = jnp.maximum(pre, 0.0) + jnp.log1p(jnp.exp(-jnp.abs(pre)))
    a = -head_ref[0:1, :] * dt
    seq = lax.broadcasted_iota(jnp.int32, (length, length), 1)
    row_id = lax.broadcasted_iota(jnp.int32, (length, length), 0)
    inside = (seq >= own) & (seq <= row_id)
    cum = dot_f32(jnp.where(inside, 1.0, 0.0), a, highest_mode)
    member_row = lax.broadcasted_iota(jnp.int32, (8, length), 0)
    member_tok = lax.broadcasted_iota(jnp.int32, (8, length), 1)
    ends = starts[1:] + [jnp.int32(length)]
    member = jnp.zeros((8, length), jnp.float32)
    for k in range(REQ_GRP):
        member = jnp.where(
            (member_row == k) & (member_tok >= starts[k]) & (member_tok < ends[k]), 1.0, member
        )
    total = dot_f32(member, a, highest_mode)
    total_decay = jnp.exp(total)
    own_total = jnp.zeros_like(a)
    for k in range(REQ_GRP):
        own_total = jnp.where((tok >= starts[k]) & (tok < ends[k]), total[k : k + 1], own_total)
    weight = jnp.exp(own_total - cum) * dt
    init_decay = jnp.exp(cum)
    cum_t = cum.T
    dt_t = dt.T
    lane_head = lax.broadcasted_iota(jnp.int32, (1, STATE_ROWS), 1) // P_SIZE
    carry = jnp.zeros((length, STATE_ROWS), jnp.float32)
    weighted = x_wide * head_lanes([weight[:, h : h + 1] for h in range(HEAD_DEV)], lane_head)
    w_high, w_low = split_bf16(weighted.T)
    for k in range(REQ_GRP):
        held = served_ref[origin_ref[k], pl.ds(0, STATE_ROWS), :]
        h_high, h_low = split_bf16(held.T)
        mine = (tok >= starts[k]) & (tok < ends[k])
        carry = jnp.where(mine, dot_f32(c_conv, h_high) + dot_f32(c_conv, h_low), carry)
        b_mine = jnp.where(mine, b_conv.astype(jnp.float32), 0.0).astype(jnp.bfloat16)
        gained = dot_f32(w_high, b_mine) + dot_f32(w_low, b_mine)
        served = jnp.where(k < total_ref[0], 1.0, 0.0)
        for h in range(HEAD_DEV):
            rows = slice(h * P_SIZE, (h + 1) * P_SIZE)
            new_ref[k, rows, :] = served * (
                total_decay[k : k + 1, h : h + 1] * held[rows] + gained[rows]
            )
    init_wide = head_lanes([init_decay[:, h : h + 1] for h in range(HEAD_DEV)], lane_head)
    base = init_wide * carry + skip_ref[...] * x_wide
    step = 256 if length % 256 == 0 else length
    for low in range(0, length, step):
        high = low + step
        scores = lax.dot_general(
            c_conv[low:high], b_conv[:high], (((1,), (1,)), ((), ())),
            preferred_element_type=jnp.float32,
        )
        scores = jnp.where(inside[low:high, :high], scores, 0.0)
        local = jnp.zeros((step, STATE_ROWS), jnp.float32)
        for h in range(HEAD_DEV):
            decay = jnp.exp(jnp.minimum(cum[low:high, h : h + 1] - cum_t[h : h + 1, :high], 0.0))
            mixing = (scores * decay * dt_t[h : h + 1, :high]).astype(jnp.bfloat16)
            local = jnp.where(lane_head == h, dot_f32(mixing, x_conv[:high]), local)
        y_ref[low:high, :] = (local + base[low:high]).astype(jnp.bfloat16)


def ssd(starts, req_total, origin, x_pre, b_cols, c_cols, dt_cols, taps, heads, skip, served):
    length = x_pre.shape[0]
    vmem = pl.BlockSpec(memory_space=pltpu.VMEM)
    smem = pl.BlockSpec(memory_space=pltpu.SMEM)
    return pl.pallas_call(
        ssd_kernel,
        out_shape=(
            jax.ShapeDtypeStruct((length, STATE_ROWS), jnp.bfloat16),
            jax.ShapeDtypeStruct((REQ_GRP, STATE_ROWS, DSTATE), jnp.float32),
        ),
        in_specs=[smem] * 3 + [vmem] * 8,
        out_specs=(vmem, vmem),
        scratch_shapes=[
            pltpu.VMEM((3, length, DSTATE), jnp.bfloat16),
        ],
        compiler_params=pltpu.CompilerParams(vmem_limit_bytes=48 * 2**20),
    )(starts, req_total, origin, x_pre, b_cols, c_cols, dt_cols, taps, heads, skip, served)


def tail_compute(
    starts, req_total, origin, x_pre, b_cols, c_cols, dt_cols, conv_x, conv_x_bias, conv_bc,
    conv_bc_bias, rate, dt_bias, dskip, bc_group, served,
):
    conv_all = jnp.concatenate([conv_bc, conv_bc_bias[None]], axis=0)
    b_taps = lax.dynamic_slice_in_dim(conv_all, bc_group * DSTATE, DSTATE, 1)
    c_taps = lax.dynamic_slice_in_dim(conv_all, (NGRP + bc_group) * DSTATE, DSTATE, 1)
    x_taps = jnp.concatenate([conv_x, conv_x_bias[None]], axis=0)
    taps = jnp.pad(jnp.concatenate([x_taps, b_taps, c_taps], axis=1), ((0, 3), (0, 0)))
    heads = jnp.pad(jnp.stack([rate, dt_bias]), ((0, 6), (0, LANES - HEAD_DEV)))
    skip = jnp.repeat(dskip, P_SIZE)[None]
    y, new = ssd(
        starts, req_total, origin, x_pre, b_cols, c_cols, dt_cols, taps, heads, skip, served
    )
    return y, new.reshape(REQ_GRP, HEAD_DEV, P_SIZE, DSTATE)


def layer_kernel(
    groups, shards, hid_ref, wx_ref, ws_ref, old_ref, xt_ref, bct_ref, cx_ref, cxb_ref, cb_ref, cbb_ref,
    rate_ref, bias_ref, dskip_ref, count_ref, source_ref, start_ref, y_ref, new_ref,
    hid_in, swap_in, w_all, bc_keep, bc_send, bc_in, bcz_send, bcz_in, bc_conv,
    xz_send, xz_in, dt_send, dt_in, pack_ref, served_in,
    hid_sem, swap_sem, two_sem, w_send, w_recv, bcy_s, bcy_r, bcz_s, bcz_r, fin_sem,
    xz_s, xz_r, dt_s, dt_r, st_s, st_r, carry_keep, mix_keep,
):
    g = lax.axis_index("group")
    s = lax.axis_index("shard")
    chips = groups // 2
    q, j = s // 2, s % 2
    x, c = g // 2, g % 2
    gx = (chips - 1 - x) * 2 + c
    gc = x * 2 + 1 - c
    other = q * 2 + 1 - j
    half = hid_ref.shape[1]
    root = (q % 2) == c

    def remote(src, dst, send, recv, to_g, to_s):
        return pltpu.make_async_remote_copy(
            src_ref=src, dst_ref=dst, send_sem=send, recv_sem=recv,
            device_id=(to_g, to_s), device_id_type=pl.DeviceIdType.MESH,
        )

    barrier = pltpu.get_barrier_semaphore()
    for d in range(1, shards):
        pl.semaphore_signal(
            barrier, inc=1, device_id=(g, (s + d) % shards), device_id_type=pl.DeviceIdType.MESH
        )
    for d in range(1, groups):
        pl.semaphore_signal(
            barrier, inc=1, device_id=((g + d) % groups, s), device_id_type=pl.DeviceIdType.MESH
        )
    pl.semaphore_wait(barrier, shards - 1 + groups - 1)

    keep = wx_ref.at[pl.ds(pl.multiple_of(x * half, half), half), :]
    give = wx_ref.at[pl.ds(pl.multiple_of((1 - x) * half, half), half), :]
    swap = remote(give, swap_in, swap_sem.at[0], swap_sem.at[1], gx, s)
    swap.start()
    first = remote(keep, w_all.at[x, q], two_sem.at[0], w_recv.at[x, q], g, g * 2 + j)
    second = remote(swap_in, w_all.at[x, q], two_sem.at[1], w_recv.at[x, q], g, gx * 2 + j)

    @pl.when(q != g)
    def _():
        first.start()

    width = DSTATE
    hid = hid_ref[...]

    def bc_block(side, i):
        low = pl.multiple_of((side * groups + i) * width, width)
        return lax.dot_general(
            hid, ws_ref[pl.ds(low, width), :], (((1,), (1,)), ((), ())),
            preferred_element_type=jnp.float32,
        )

    def bcy(i):
        return remote(bc_send.at[i], bc_in.at[i], bcy_s.at[i], bcy_r.at[i], g, other)

    @pl.loop(0, groups)
    def _(i):
        bc_send[i] = bc_block(1 - j, i).astype(jnp.bfloat16)
        bcy(i).start()

    hidden_copy = remote(hid_ref, hid_in, hid_sem.at[0], hid_sem.at[1], g, other)
    hidden_copy.start()
    dt_part = lax.dot_general(
        ws_ref[pl.ds(2 * NGRP * DSTATE, HEAD_DEV * shards), :], hid, (((1,), (1,)), ((), ())), preferred_element_type=jnp.float32
    )
    for o in range(shards):
        part = dt_part[o * HEAD_DEV : (o + 1) * HEAD_DEV]
        dt_send[o] = jnp.concatenate([part, jnp.zeros((8 - HEAD_DEV, part.shape[1]), jnp.float32)], 0)

    def dt_copy(d):
        to = (s + d) % shards
        return remote(dt_send.at[to], dt_in.at[d], dt_s.at[d], dt_r.at[d], g, to)

    for d in range(1, shards):
        dt_copy(d).start()
    swap.wait_recv()

    @pl.when(q != gx)
    def _():
        second.start()

    @pl.when(q == g)
    def _():
        w_all[x, q] = wx_ref[pl.ds(pl.multiple_of(x * half, half), half), :]

    @pl.when(q == gx)
    def _():
        w_all[x, q] = swap_in[...]

    def to_chip(p):
        return remote(w_all.at[x, p], w_all.at[x, p], w_send.at[2, p], w_recv.at[x, p], gx, s)

    def to_core(u, p):
        return remote(w_all.at[u, p], w_all.at[u, p], w_send.at[u, p], w_recv.at[u, p], gc, s)

    @pl.when(root)
    def _():
        to_chip(q).start()
        to_core(x, q).start()

    def state(d):
        to = (g + d) % groups
        return remote(pack_ref.at[to], served_in.at[g], st_s.at[d], st_r.at[d], to, s)

    def state_from(d):
        frm = (g + groups - d) % groups
        return remote(pack_ref.at[frm], served_in.at[frm], st_s.at[d], st_r.at[d], frm, s)

    bc_group = s * NGRP // shards
    places = old_ref.shape[0]
    for d in range(groups):
        wanted = jnp.int32(0)
        for k in range(REQ_GRP):
            named = source_ref[d, k]
            wanted = wanted + jnp.where(named // places == g, named % places, 0)
        pack_ref[d, 0:STATE_ROWS, :] = old_ref[wanted]
        for i in range(KCONV - 1):
            at = STATE_ROWS + i
            pack_ref[d, at : at + 1, :] = xt_ref[i, pl.ds(wanted, 1), :]
        for side in range(2):
            low = pl.multiple_of((side * NGRP + bc_group) * DSTATE, DSTATE)
            at = STATE_ROWS + 8 * (side + 1)
            for i in range(KCONV - 1):
                pack_ref[d, at + i : at + i + 1, :] = bct_ref[i, pl.ds(wanted, 1), pl.ds(low, DSTATE)]
        for block in range(3):
            at = STATE_ROWS + 8 * block
            pack_ref[d, at + 3 : at + 8, :] = jnp.zeros((5, DSTATE), jnp.float32)
    for d in range(1, groups):
        state(d).start()

    @pl.loop(0, groups)
    def _(i):
        bc_keep[i] = bc_block(j, i)

    def bcz(d):
        to = (q + d) % groups
        return remote(bcz_send.at[d], bcz_in.at[d], bcz_s.at[d], bcz_r.at[d], g, to * 2 + j)

    @pl.loop(0, groups)
    def _(i):
        bcy(i).wait_recv()

    @pl.loop(1, groups)
    def _(d):
        to = (q + d) % groups
        bcz_send[d] = (bc_keep[to] + bc_in[to].astype(jnp.float32)).astype(jnp.bfloat16)
        bcz(d).start()

    def pass_on(p):
        to_core(1 - x, p).wait_recv()
        to_core(1 - x, p).start()

    @pl.when(root)
    def _():
        @pl.loop(1, groups)
        def _(d):
            p = (q + groups - d) % groups
            to_core(x, p).wait_recv()
            to_chip(p).start()
            to_core(x, p).start()

        pass_on(q)

    hidden_copy.wait_recv()

    def xz(d):
        to = (q + groups - d) % groups
        return remote(xz_send.at[d], xz_in.at[d], xz_s.at[d], xz_r.at[d], g, to * 2 + j)

    def x_block(p):
        @pl.when(jnp.logical_not(root))
        def _():
            to_core(0, p).wait_recv()
            to_core(1, p).wait_recv()

        return dot_f32(hid_ref[...], w_all[j, p]) + dot_f32(hid_in[...], w_all[1 - j, p])

    @pl.loop(1, groups)
    def _(d):
        p = (q + groups - d) % groups

        @pl.when(root)
        def _():
            pass_on(p)

        xz_send[d] = x_block(p).astype(jnp.bfloat16)
        xz(d).start()

    total_x = x_block(q)
    @pl.loop(1, groups)
    def _(d):
        bcz(d).wait_recv()

    mine = bc_keep[q] + bc_in[q].astype(jnp.float32)
    for d in range(1, groups):
        mine = mine + bcz_in[d].astype(jnp.float32)
    length = hid_ref.shape[0]
    origin = [source_ref[g, k] // places for k in range(REQ_GRP)]
    starts = [start_ref[g, k] for k in range(REQ_GRP)]
    tok = lax.broadcasted_iota(jnp.int32, (length, 1), 0)
    own = jnp.zeros((length, 1), jnp.int32)
    for k in range(1, REQ_GRP):
        own = jnp.where(tok >= starts[k], starts[k], own)
    place = tok - own
    slot = lax.broadcasted_iota(jnp.int32, (length, TAIL_ROWS), 1)
    hot = jnp.zeros((length, TAIL_ROWS), jnp.float32)
    for k in range(REQ_GRP):
        for i in range(KCONV - 1):
            hot = jnp.where((slot == 3 * k + i) & (tok == starts[k] + i) & (place == i), 1.0, hot)

    def convolve(values, tap, bias, block):
        taps = [tap[i : i + 1] for i in range(KCONV)]
        rows = []
        for k in range(REQ_GRP):
            low = pl.multiple_of(STATE_ROWS + 8 * block, 8)
            tail = served_in[origin[k], pl.ds(low, 8), :]
            for i in range(KCONV - 1):
                row = jnp.zeros((1, DSTATE), jnp.float32)
                for lag in range(i + 1, KCONV):
                    at = KCONV - 1 - lag + i
                    row = row + taps[KCONV - 1 - lag] * tail[at : at + 1]
                rows.append(row)
        rows.append(jnp.zeros((TAIL_ROWS - len(rows), DSTATE), jnp.float32))
        summed = taps[KCONV - 1] * values + dot_f32(hot, jnp.concatenate(rows, 0), highest_mode)
        for lag in range(1, KCONV):
            shifted = pltpu.roll(values, lag, 0)
            summed = summed + taps[KCONV - 1 - lag] * jnp.where(place >= lag, shifted, 0.0)
        summed = summed + bias
        return (summed * jax.nn.sigmoid(summed)).astype(jnp.bfloat16)

    served_in[g] = pack_ref[g]
    for d in range(1, groups):
        state_from(d).wait_recv()
    side_cols = pl.ds(pl.multiple_of((j * NGRP + bc_group) * DSTATE, DSTATE), DSTATE)
    bc_conv[j] = convolve(mine, cb_ref[:, side_cols], cbb_ref[:, side_cols], j + 1)
    final = remote(bc_conv.at[j], bc_conv.at[j], fin_sem.at[0], fin_sem.at[1], g, other)
    final_in = remote(bc_conv.at[1 - j], bc_conv.at[1 - j], fin_sem.at[0], fin_sem.at[1], g, other)
    final.start()
    dt_sum = dt_send[s]
    for d in range(1, shards):
        dt_copy(d).wait_recv()
        dt_sum = dt_sum + dt_in[d]
    steps = jnp.concatenate([dt_sum, jnp.zeros((LANES - 8, length), jnp.float32)], 0)
    lane = lax.broadcasted_iota(jnp.int32, (1, LANES), 1)
    lane_head = lax.broadcasted_iota(jnp.int32, (1, STATE_ROWS), 1) // P_SIZE
    rate_row = jnp.zeros((1, LANES), jnp.float32)
    bias_row = jnp.zeros((1, LANES), jnp.float32)
    skip_row = jnp.zeros((1, STATE_ROWS), jnp.float32)
    for h in range(HEAD_DEV):
        rate_row = jnp.where(lane == h, rate_ref[h], rate_row)
        bias_row = jnp.where(lane == h, bias_ref[h], bias_row)
        skip_row = jnp.where(lane_head == h, dskip_ref[h], skip_row)
    pre = steps.T + bias_row
    dt = jnp.maximum(pre, 0.0) + jnp.log1p(jnp.exp(-jnp.abs(pre)))
    a = -rate_row * dt
    seq = lax.broadcasted_iota(jnp.int32, (length, length), 1)
    row_id = lax.broadcasted_iota(jnp.int32, (length, length), 0)
    inside = (seq >= own) & (seq <= row_id)
    cum = dot_f32(jnp.where(inside, 1.0, 0.0), a, highest_mode)
    member_row = lax.broadcasted_iota(jnp.int32, (8, length), 0)
    member_tok = lax.broadcasted_iota(jnp.int32, (8, length), 1)
    ends = starts[1:] + [jnp.int32(length)]
    member = jnp.zeros((8, length), jnp.float32)
    for k in range(REQ_GRP):
        member = jnp.where(
            (member_row == k) & (member_tok >= starts[k]) & (member_tok < ends[k]), 1.0, member
        )
    total = dot_f32(member, a, highest_mode)
    total_decay = jnp.exp(total)
    own_total = jnp.zeros_like(a)
    for k in range(REQ_GRP):
        own_total = jnp.where((tok >= starts[k]) & (tok < ends[k]), total[k : k + 1], own_total)
    weight = jnp.exp(own_total - cum) * dt
    init_decay = jnp.exp(cum)
    cum_t = cum.T
    dt_t = dt.T
    final_in.wait_recv()
    b_conv, c_conv = bc_conv[0], bc_conv[1]
    carry = jnp.zeros((length, STATE_ROWS), jnp.float32)
    for k in range(REQ_GRP):
        h_high, h_low = split_bf16(served_in[origin[k], pl.ds(0, STATE_ROWS), :].T)
        mine_tok = (tok >= starts[k]) & (tok < ends[k])
        carry = jnp.where(mine_tok, dot_f32(c_conv, h_high) + dot_f32(c_conv, h_low), carry)
    init_wide = head_lanes([init_decay[:, h : h + 1] for h in range(HEAD_DEV)], lane_head)
    carry_keep[...] = init_wide * carry
    step = 256 if length % 256 == 0 else length
    for low in range(0, length, step):
        high = low + step
        scores = lax.dot_general(
            c_conv[low:high], b_conv[:high], (((1,), (1,)), ((), ())),
            preferred_element_type=jnp.float32,
        )
        scores = jnp.where(inside[low:high, :high], scores, 0.0)
        for h in range(HEAD_DEV):
            decay = jnp.exp(jnp.minimum(cum[low:high, h : h + 1] - cum_t[h : h + 1, :high], 0.0))
            mix_keep[h, low:high, :high] = (scores * decay * dt_t[h : h + 1, :high]).astype(jnp.bfloat16)
    for d in range(1, groups):
        xz(d).wait_recv()
        total_x = total_x + xz_in[d].astype(jnp.float32)
    x_pre = total_x.astype(jnp.bfloat16).astype(jnp.float32)
    x_conv = convolve(x_pre, cx_ref[...], cxb_ref[...], 0)
    x_wide = x_conv.astype(jnp.float32)
    weighted = x_wide * head_lanes([weight[:, h : h + 1] for h in range(HEAD_DEV)], lane_head)
    w_high, w_low = split_bf16(weighted.T)
    for k in range(REQ_GRP):
        held = served_in[origin[k], pl.ds(0, STATE_ROWS), :]
        mine = (tok >= starts[k]) & (tok < ends[k])
        b_mine = jnp.where(mine, b_conv.astype(jnp.float32), 0.0).astype(jnp.bfloat16)
        gained = dot_f32(w_high, b_mine) + dot_f32(w_low, b_mine)
        served = jnp.where(k < count_ref[g], 1.0, 0.0)
        for h in range(HEAD_DEV):
            rows = slice(h * P_SIZE, (h + 1) * P_SIZE)
            new_ref[k, rows, :] = served * (
                total_decay[k : k + 1, h : h + 1] * held[rows] + gained[rows]
            )
    base = carry_keep[...] + skip_row * x_wide
    for low in range(0, length, step):
        high = low + step
        local = jnp.zeros((step, STATE_ROWS), jnp.float32)
        for h in range(HEAD_DEV):
            mixed = dot_f32(mix_keep[h, low:high, :high], x_conv[:high])
            local = jnp.where(lane_head == h, mixed, local)
        y_ref[low:high, :] = (local + base[low:high]).astype(jnp.bfloat16)

    swap.wait_send()
    hidden_copy.wait_send()
    final.wait_send()

    @pl.when(q != g)
    def _():
        first.wait_send()

    @pl.when(q != gx)
    def _():
        second.wait_send()

    @pl.when(root)
    def _():
        @pl.loop(0, groups)
        def _(p):
            to_chip(p).wait_send()
            to_core(0, p).wait_send()
            to_core(1, p).wait_send()

    @pl.loop(0, groups)
    def _(i):
        bcy(i).wait_send()

    for d in range(1, groups):
        bcz(d).wait_send()
        xz(d).wait_send()
        state(d).wait_send()
    for d in range(1, shards):
        dt_copy(d).wait_send()


def layer(
    groups, shards, hidden, w_x, w_small, conv_x, conv_x_bias, conv_bc, conv_bc_bias, rate,
    dt_bias, dskip, old_state, x_tail, bc_tail, req_count, req_source, req_start,
):
    length, half = hidden.shape
    width = w_x.shape[1]
    places = old_state.shape[0]
    vmem = pl.BlockSpec(memory_space=pltpu.VMEM)
    smem = pl.BlockSpec(memory_space=pltpu.SMEM)
    bf16, f32 = jnp.bfloat16, jnp.float32
    dma = pltpu.SemaphoreType.DMA
    packed = (groups, STATE_ROWS + 24, DSTATE)
    y, new = pl.pallas_call(
        functools.partial(layer_kernel, groups, shards),
        out_shape=(
            jax.ShapeDtypeStruct((length, STATE_ROWS), bf16),
            jax.ShapeDtypeStruct((REQ_GRP, STATE_ROWS, DSTATE), f32),
        ),
        in_specs=[vmem] * 10 + [smem] * 6,
        out_specs=(vmem, vmem),
        scratch_shapes=[
            pltpu.VMEM((length, half), bf16),
            pltpu.VMEM((half, width), bf16),
            pltpu.VMEM((2, groups, half, width), bf16),
            pltpu.VMEM((groups, length, DSTATE), f32),
            pltpu.VMEM((groups, length, DSTATE), bf16),
            pltpu.VMEM((groups, length, DSTATE), bf16),
            pltpu.VMEM((groups, length, DSTATE), bf16),
            pltpu.VMEM((groups, length, DSTATE), bf16),
            pltpu.VMEM((2, length, DSTATE), bf16),
            pltpu.VMEM((groups, length, width), bf16),
            pltpu.VMEM((groups, length, width), bf16),
            pltpu.VMEM((shards, 8, length), f32),
            pltpu.VMEM((shards, 8, length), f32),
            pltpu.VMEM(packed, f32),
            pltpu.VMEM(packed, f32),
            dma((2,)), dma((2,)), dma((2,)), dma((3, groups)), dma((2, groups)),
            dma((groups,)), dma((groups,)), dma((groups,)), dma((groups,)), dma((2,)),
            dma((groups,)), dma((groups,)), dma((shards,)), dma((shards,)),
            dma((groups,)), dma((groups,)),
            pltpu.VMEM((length, STATE_ROWS), f32),
            pltpu.VMEM((HEAD_DEV, length, length), bf16),
        ],
        compiler_params=pltpu.CompilerParams(
            collective_id=0, has_side_effects=True, vmem_limit_bytes=58 * 2**20
        ),
    )(
        hidden, w_x, w_small.T, old_state.reshape(places, STATE_ROWS, DSTATE),
        jnp.transpose(x_tail, (1, 0, 2)), jnp.transpose(bc_tail, (1, 0, 2)),
        conv_x, conv_x_bias[None], conv_bc, conv_bc_bias[None], rate, dt_bias, dskip,
        req_count, req_source, req_start,
    )
    return y, new.reshape(REQ_GRP, HEAD_DEV, P_SIZE, DSTATE)


def packed_states(old_state, x_tail, bc_tail, req_source, bc_group):
    places = old_state.shape[0]
    me = lax.axis_index("group")
    home = req_source // places
    wanted = jnp.sum(jnp.where(home == me, req_source % places, 0), axis=1)
    b_tail = lax.dynamic_slice_in_dim(bc_tail, bc_group * DSTATE, DSTATE, 2)
    c_tail = lax.dynamic_slice_in_dim(bc_tail, (NGRP + bc_group) * DSTATE, DSTATE, 2)
    tails = [jnp.pad(t, ((0, 0), (0, 5), (0, 0))) for t in (x_tail, b_tail, c_tail)]
    flat = jnp.concatenate([old_state.reshape(places, STATE_ROWS, DSTATE)] + tails, axis=1)
    picked = [
        lax.dynamic_index_in_dim(flat, wanted[d], 0, keepdims=False)
        for d in range(wanted.shape[0])
    ]
    return jnp.stack(picked), home


def small_columns(hidden, w_small):
    length = hidden.shape[0]
    shards = lax.axis_size("shard")
    per = shards // NGRP
    width = 2 * DSTATE // per
    partial = jnp.dot(hidden, w_small, preferred_element_type=jnp.float32)
    b_part = partial[:, : NGRP * DSTATE].reshape(length, NGRP, DSTATE)
    c_part = partial[:, NGRP * DSTATE : 2 * NGRP * DSTATE].reshape(length, NGRP, DSTATE)
    bc = jnp.concatenate([b_part, c_part], axis=2).reshape(length, shards, width)
    dt = partial[:, 2 * NGRP * DSTATE :].reshape(length, shards, HEAD_DEV)
    dt_rows = jnp.transpose(dt, (1, 2, 0)).reshape(shards, HEAD_DEV * length // width, width)
    pack = jnp.concatenate([jnp.transpose(bc, (1, 0, 2)), dt_rows], axis=1)
    mine = lax.psum_scatter(pack, "shard", scatter_dimension=0, tiled=False)
    groups = [[q * per + r for r in range(per)] for q in range(NGRP)]
    both = lax.all_gather(mine[:length], "shard", axis_index_groups=groups, axis=1, tiled=True)
    dt_mine = mine[length:].reshape(HEAD_DEV, length)
    return both[:, :DSTATE], both[:, DSTATE:], jnp.pad(dt_mine, ((0, 8 - HEAD_DEV), (0, 0)))


def body(
    hidden, w_x, w_small, conv_x, conv_x_bias, conv_bc, conv_bc_bias, rate, dt_bias, dskip,
    old_state, x_tail, bc_tail, req_count, req_source, req_start,
):
    shards = lax.axis_size("shard")
    groups = lax.axis_size("group")
    if groups == NGRP and shards == 2 * groups:
        return layer(
            groups, shards, hidden, w_x, w_small, conv_x, conv_x_bias, conv_bc, conv_bc_bias, rate,
            dt_bias, dskip, old_state, x_tail, bc_tail, req_count, req_source, req_start,
        )
    heads_grp = HEAD_DEV * shards // NGRP
    group_index = lax.axis_index("group")
    bc_group = lax.axis_index("shard") * HEAD_DEV // heads_grp
    starts = lax.dynamic_index_in_dim(req_start, group_index, 0, keepdims=False)
    req_total = lax.dynamic_slice_in_dim(req_count, group_index, 1, 0)
    pack, home = packed_states(old_state, x_tail, bc_tail, req_source, bc_group)
    origin = lax.dynamic_index_in_dim(home, group_index, 0, keepdims=False)
    served = lax.all_to_all(pack, "group", split_axis=0, concat_axis=0, tiled=True)
    b_cols, c_cols, dt_cols = small_columns(hidden, w_small)
    panel = lax.all_gather(w_x, "group", axis=0, tiled=True)
    rows = lax.all_gather(hidden, "shard", axis=1, tiled=True)
    x_pre = jnp.dot(rows, panel, preferred_element_type=jnp.float32).astype(jnp.bfloat16)
    y, new = tail_compute(
        starts, req_total, origin, x_pre, b_cols, c_cols, dt_cols, conv_x, conv_x_bias, conv_bc,
        conv_bc_bias, rate, dt_bias, dskip, bc_group, served,
    )
    return y, new


def solution(mesh):
    in_specs = (
        P("group", "shard"),
        P("group", "shard"),
        P("shard", None),
        P(None, "shard"),
        P("shard"),
        P(),
        P(),
        P("shard"),
        P("shard"),
        P("shard"),
        P("group", "shard", None, None),
        P("group", None, "shard"),
        P("group", None, None),
        P(),
        P(),
        P(),
    )
    out_specs = (P("group", "shard"), P("group", "shard", None, None))
    return jax.shard_map(body, mesh=mesh, in_specs=in_specs, out_specs=out_specs, check_vma=False)
```
